256 devices in a mesh: dp: 32 (over x_hi, z, core), mp: 8 (over x_lo, y).
Axes of the slice: x: 4 (x_hi: 2, x_lo: 2; x = x_hi * 2 + x_lo), y: 4, z: 8, core: 2. Of those that a mesh axis runs over, the one named last changes fastest.
Arguments:
- image_emb: bfloat16 [16384, 1152], P(('dp', 'mp')), may hold values from -0.1796875 to 0.1796875
- text_emb: bfloat16 [16384, 1152], P(('dp', 'mp')), may hold values from -0.1796875 to 0.1796875
- log_temp: float32 [1], replicated, may hold values from 1.6 to 2.7
- bias: float32 [1], replicated, may hold values from -3 to -1
Outputs:
- image_grad: float32 [16384, 1152], P(('dp', 'mp'))
- text_grad: float32 [16384, 1152], P(('dp', 'mp'))
The draws below stay inside these ranges and needn't reach their ends.
All inputs are finite; a program needn't handle non-finite values.
Results may differ from the reference program's by a relative error of at most 0.0057.
Values may be sent and summed in bfloat16 or wider, within the bound.
A program may use at most 64 MiB of HBM per device.

```python
import jax
import jax.numpy as jnp
from jax import lax

E = 1152
BATCH = 16384
N_DP = 32


def levels(key, extent, split, low, largest):
    def one(axis_at, parts):
        steps = jax.random.uniform(jax.random.fold_in(jax.random.fold_in(key, 6), axis_at), (parts,), jnp.float32, low / len(split), largest / len(split))
        return jnp.repeat(jnp.exp(steps), extent[axis_at] // parts).reshape((-1,) + (1,) * (len(extent) - axis_at - 1))

    loudness = one(*split[0])
    for cut in split[1:]:
        loudness = loudness * one(*cut)
    return loudness


def normal_values(stream_key, extent, scale, reach, shards=(), kind=jnp.bfloat16):
    result = scale * jax.random.normal(stream_key, extent, jnp.float32)
    if shards:
        result = result * levels(stream_key, extent, shards, -0.22, 0.18)
    return jnp.clip(result, -reach, reach).astype(kind)


def setup_inputs(seed: int = 0) -> dict:
    key_list = jax.random.split(jax.random.key(seed), 5)
    image_emb = normal_values(key_list[0], (BATCH, E), 0.03, 0.1796875, ((0, 256),))
    text_emb = normal_values(key_list[1], (BATCH, E), 0.03, 0.1796875, ((0, 256),))
    log_temp = jnp.clip(jax.random.uniform(key_list[2], (1,), jnp.float32, 1.6, 2.7), 1.6, 2.7)
    bias = jnp.clip(jax.random.uniform(key_list[3], (1,), jnp.float32, -3.0, -1.0), -3.0, -1.0)
    return dict(image_emb=image_emb, text_emb=text_emb, log_temp=log_temp, bias=bias)


eps = 1e-06

def normalize(emb):
    wide = emb.astype(jnp.float32)
    inverse = lax.rsqrt(lax.optimization_barrier(jnp.sum(wide * wide, axis=1, keepdims=True)) + eps)
    return (wide * inverse, inverse)

def back_norm(unit, inverse, grad):
    return inverse * (grad - unit * lax.optimization_barrier(jnp.sum(unit * grad, axis=1, keepdims=True)))

def reference(image_emb, text_emb, log_temp, bias):
    tau = jnp.exp(log_temp[0])
    shift_b = bias[0]
    unit_img, inv_img = normalize(image_emb)
    unit_txt, inv_txt = normalize(text_emb)
    p_all = unit_img.astype(jnp.bfloat16)
    q_all = unit_txt.astype(jnp.bfloat16)
    total = p_all.shape[0]
    width = p_all.shape[1]
    group = total // N_DP
    img_index = jnp.arange(total, dtype=jnp.int32)
    q_blocks = q_all.reshape(N_DP, group, width)

    def step(grad_p, inputs):
        q_blk, block = inputs
        txt_index = block * group + jnp.arange(group, dtype=jnp.int32)
        scores = lax.dot_general(q_blk, p_all, (((1,), (1,)), ((), ())), preferred_element_type=jnp.float32)
        logits = tau * scores + shift_b
        label = jnp.where(txt_index[:, None] == img_index[None, :], jnp.float32(1.0), jnp.float32(-1.0))
        coef = (-tau * label * jax.nn.sigmoid(-label * logits)).astype(jnp.bfloat16)
        grad_q = jnp.dot(coef, p_all, preferred_element_type=jnp.float32)
        grad_p = grad_p + lax.dot_general(coef, q_blk, (((0,), (0,)), ((), ())), preferred_element_type=jnp.float32)
        return (grad_p, grad_q)
    start = jnp.zeros((total, width), jnp.float32)
    grad_p, grad_qs = lax.scan(step, start, (q_blocks, jnp.arange(N_DP, dtype=jnp.int32)))
    grad_q = grad_qs.reshape(total, width)
    return (back_norm(unit_img, inv_img, grad_p), back_norm(unit_txt, inv_txt, grad_q))
```

```python
import functools

import jax
import jax.numpy as jnp
from jax import lax
from jax.experimental import pallas as pl
from jax.experimental.pallas import tpu as pltpu
from jax.sharding import PartitionSpec as P

EPS = 1e-06
MESH = pl.DeviceIdType.MESH
NX, NY, NZ = 4, 4, 8
ROWS = 64
HALF = ROWS // 2
QUARTER = ROWS // 4
NT = (((1,), (1,)), ((), ()))
TN = (((0,), (0,)), ((), ()))
NN = (((1,), (0,)), ((), ()))

IMG_SLOTS = [
    (0, 0), (1, 0), (3, 0), (0, 1), (0, 3), (2, 0),
    (1, 1), (1, 3), (3, 1), (3, 3), (0, 2), (2, 1),
    (2, 3), (1, 2), (3, 2), (2, 2),
]
TXT_SLOTS = [(dz, s) for dz in (0, 1, 7, 2, 6, 3, 5, 4) for s in (0, 1)]


class Edge:
    def __init__(self, src, dst, row, count, axis, sign):
        self.src, self.dst, self.row, self.count = src, dst, row, count
        self.axis, self.sign = axis, sign


def img_edges():
    edges = {}
    for half, first, second in (("A", "x", "y"), ("B", "y", "x")):
        base = 0 if half == "A" else HALF

        def at(df, ds, first=first):
            return (df % 4, ds % 4) if first == "x" else (ds % 4, df % 4)

        for sg in (1, -1):
            quarter = base + (0 if sg == 1 else QUARTER)
            edges[half, "f", sg] = Edge(at(0, 0), at(-sg, 0), base, HALF, first, sg)
            edges[half, "fq", sg] = Edge(at(-sg, 0), at(2, 0), quarter, QUARTER, first, sg)
            for df in range(4):
                edges[half, "s", df, sg] = Edge(at(df, 0), at(df, -sg), base, HALF, second, sg)
                edges[half, "sq", df, sg] = Edge(at(df, -sg), at(df, 2), quarter, QUARTER, second, sg)
    return edges


def txt_edges():
    edges = {}
    for sg in (1, -1):
        for k in range(3):
            edges["z", k, sg] = Edge(((-sg * k) % NZ, 0), ((-sg * (k + 1)) % NZ, 0), 0, ROWS, "z", sg)
        edges["z", 3, sg] = Edge(
            ((-sg * 3) % NZ, 0), (4, 0), 0 if sg == 1 else HALF, HALF, "z", sg
        )
    for dz in range(NZ):
        edges["c", dz] = Edge((dz, 0), (dz, 1), 0, ROWS, "c", 1)
    return edges


class Side:
    def __init__(self, slots, edges, rows, part, out, back, sems, place):
        self.at = {slot: i * ROWS for i, slot in enumerate(slots)}
        self.edges = edges
        self.number = {key: i for i, key in enumerate(edges)}
        self.rows, self.part, self.out, self.back = rows, part, out, back
        self.g_send, self.g_recv, self.r_send, self.r_recv = sems
        self.place = place
        self.sent, self.returned = set(), set()
        self.seen, self.taken = set(), set()

    def span(self, slot, row, count):
        return pl.ds(self.at[slot] + row, count)

    def gather_copy(self, key):
        e, i = self.edges[key], self.number[key]
        return pltpu.make_async_remote_copy(
            src_ref=self.rows.at[self.span(e.src, e.row, e.count)],
            dst_ref=self.rows.at[self.span(e.dst, e.row, e.count)],
            send_sem=self.g_send.at[i],
            recv_sem=self.g_recv.at[i],
            device_id=self.place(e.axis, e.sign),
            device_id_type=MESH,
        )

    def scatter_copy(self, key):
        e, i = self.edges[key], self.number[key]
        where = self.span(e.dst, e.row, e.count)
        return pltpu.make_async_remote_copy(
            src_ref=self.out.at[where],
            dst_ref=self.back.at[where],
            send_sem=self.r_send.at[i],
            recv_sem=self.r_recv.at[i],
            device_id=self.place(e.axis, -e.sign),
            device_id_type=MESH,
        )

    def send(self, *keys):
        for key in keys:
            e = self.edges[key]
            self.arrive(e.src, e.row, e.count)
            self.gather_copy(key).start()
            self.sent.add(key)

    def arrive(self, slot, row=0, count=ROWS):
        for key, e in self.edges.items():
            if e.dst == slot and e.row < row + count and row < e.row + e.count and key not in self.seen:
                assert key in self.sent, key
                self.gather_copy(key).wait_recv()
                self.seen.add(key)

    def total(self, slot, row, count):
        value = self.part[self.span(slot, row, count), :]
        for key, e in self.edges.items():
            if e.src == slot and e.row <= row and row + count <= e.row + e.count:
                if key not in self.taken:
                    assert key in self.returned, key
                    self.scatter_copy(key).wait_recv()
                    self.taken.add(key)
                value = value + self.back[self.span(e.dst, row, count), :].astype(jnp.float32)
        return value

    def give(self, *keys):
        for key in keys:
            e = self.edges[key]
            for row in range(e.row, e.row + e.count, QUARTER):
                self.out[self.span(e.dst, row, QUARTER), :] = self.total(e.dst, row, QUARTER).astype(jnp.bfloat16)
            self.scatter_copy(key).start()
            self.returned.add(key)

    def finish(self):
        assert len(self.sent) == len(self.returned) == len(self.seen) == len(self.taken) == len(self.edges)
        for key in self.edges:
            self.gather_copy(key).wait_send()
            self.scatter_copy(key).wait_send()


def unit_of(emb):
    wide = emb.astype(jnp.float32)
    inverse = lax.rsqrt(jnp.sum(wide * wide, axis=1, keepdims=True) + EPS)
    return wide * inverse, inverse


def back_norm(unit, inverse, grad):
    return inverse * (grad - unit * jnp.sum(unit * grad, axis=1, keepdims=True))


def kernel(
    img_ref, txt_ref, temp_ref, bias_ref, img_out, txt_out,
    p_rows, q_rows, coef, p_part, q_part, p_send, q_send, p_back, q_back,
    pg_send, pg_recv, pr_send, pr_recv, qg_send, qg_recv, qr_send, qr_recv,
):
    dp, mp = lax.axis_index("dp"), lax.axis_index("mp")
    core, z, x = dp % 2, (dp // 2) % NZ, (dp // (2 * NZ)) * 2 + mp // NY
    y = mp % NY

    def place(axis, sign):
        nx, ny, nz, nc = x, y, z, core
        if axis == "x":
            nx = (x + sign + NX) % NX
        elif axis == "y":
            ny = (y + sign + NY) % NY
        elif axis == "z":
            nz = (z + sign + NZ) % NZ
        else:
            nc = 1 - core
        return ((nx // 2) * (2 * NZ) + nz * 2 + nc, (nx % 2) * NY + ny)

    barrier = pltpu.get_barrier_semaphore()
    neighbours = [place(a, s) for a in "xyz" for s in (1, -1)] + [place("c", 1)]
    for device in neighbours:
        pl.semaphore_signal(barrier, inc=1, device_id=device, device_id_type=MESH)

    img = Side(IMG_SLOTS, img_edges(), p_rows, p_part, p_send, p_back,
               (pg_send, pg_recv, pr_send, pr_recv), place)
    txt = Side(TXT_SLOTS, txt_edges(), q_rows, q_part, q_send, q_back,
               (qg_send, qg_recv, qr_send, qr_recv), place)

    half_tau = 0.5 * jnp.exp(jnp.full((1, 1), temp_ref[0], jnp.float32))
    half_bias = 0.5 * jnp.full((1, 1), bias_ref[0], jnp.float32)

    p_rows[0:ROWS, :] = unit_of(img_ref[...])[0].astype(jnp.bfloat16)
    q_rows[0:ROWS, :] = unit_of(txt_ref[...])[0].astype(jnp.bfloat16)
    pl.semaphore_wait(barrier, len(neighbours))

    def scores(t0, tn, i0, n):
        dots = lax.dot_general(q_rows[t0:t0 + tn, :], p_rows[i0:i0 + n, :], NT,
                               preferred_element_type=jnp.float32)
        wave = jnp.tanh(half_tau * dots + half_bias)
        coef[t0:t0 + tn, i0:i0 + n] = (half_tau * wave + half_tau).astype(jnp.bfloat16)

    def own_scores():
        dots = lax.dot_general(q_rows[0:ROWS, :], p_rows[0:128, :], NT,
                               preferred_element_type=jnp.float32)
        wave = jnp.tanh(half_tau * dots + half_bias)
        same = lax.broadcasted_iota(jnp.int32, dots.shape, 0) == lax.broadcasted_iota(jnp.int32, dots.shape, 1)
        coef[0:ROWS, 0:128] = (half_tau * wave + jnp.where(same, -half_tau, half_tau)).astype(jnp.bfloat16)

    def img_grads(i0, n):
        p_part[i0:i0 + n, :] = lax.dot_general(coef[:, i0:i0 + n], q_rows[...], TN,
                                               preferred_element_type=jnp.float32)

    def txt_grads(t0, n):
        q_part[t0:t0 + n, :] = lax.dot_general(coef[t0:t0 + n, :], p_rows[...], NN,
                                               preferred_element_type=jnp.float32)

    both = (1, -1)
    for sg in both:
        img.send(("A", "f", sg))
        img.send(("B", "f", sg))
        txt.send(("z", 0, sg))
    for sg in both:
        img.send(("A", "s", 0, sg))
        img.send(("B", "s", 0, sg))
    txt.send(("c", 0))
    for sg in both:
        for half in "AB":
            img.send((half, "fq", sg))
            img.send((half, "s", -sg % 4, 1), (half, "s", -sg % 4, -1))
    for sg in both:
        txt.send(("z", 1, sg))
        txt.send(("c", -sg % NZ))
    for sg in both:
        for half in "AB":
            img.send((half, "sq", 0, sg))
    for half in "AB":
        for sg in both:
            img.send((half, "s", 2, sg))
    for slot in IMG_SLOTS[:6]:
        img.arrive(slot)
    for slot in TXT_SLOTS[:6]:
        txt.arrive(slot)
    scores(0, 384, 0, 384)
    own_scores()
    for sg in both:
        txt.send(("z", 2, sg))
        txt.send(("c", -2 * sg % NZ))
    for df in (1, 3):
        for sg in both:
            for half in "AB":
                img.send((half, "sq", df, sg))
    for slot in TXT_SLOTS[6:10]:
        txt.arrive(slot)
    scores(384, 256, 0, 384)
    for sg in both:
        txt.send(("z", 3, sg))
        txt.send(("c", -3 * sg % NZ))
    for sg in both:
        for half in "AB":
            img.send((half, "sq", 2, sg))
    for slot in IMG_SLOTS[6:12]:
        img.arrive(slot)
    scores(0, 640, 384, 384)
    for slot in TXT_SLOTS[10:14]:
        txt.arrive(slot)
    scores(640, 256, 0, 768)
    txt.send(("c", 4))
    for slot in IMG_SLOTS[12:]:
        img.arrive(slot)
    scores(0, 896, 768, 256)
    for slot in TXT_SLOTS[14:]:
        txt.arrive(slot)
    scores(896, 128, 0, 1024)

    img_grads(768, 256)
    for half in "AB":
        for sg in both:
            img.give((half, "sq", 2, sg))
    for sg in both:
        img.give(("A", "sq", 1, sg), ("A", "sq", 3, sg))
    for sg in both:
        img.give(("B", "sq", 3, sg))
    txt_grads(640, 384)
    for dz in (4, 3, 5):
        txt.give(("c", dz))
    img_grads(384, 384)
    for sg in both:
        img.give(("B", "sq", 1, sg), ("A", "sq", 0, sg))
    for sg in both:
        txt.give(("z", 3, sg))
    for half in "AB":
        for sg in both:
            img.give((half, "s", 2, sg))
    txt_grads(384, 256)
    for dz in (2, 6):
        txt.give(("c", dz))
    for half in "AB":
        for sg in both:
            img.give((half, "s", 1, sg), (half, "s", 3, sg))
    for sg in both:
        txt.give(("z", 2, sg))
    img_grads(0, 384)
    for sg in both:
        img.give(("B", "sq", 0, sg))
    for half in "AB":
        for sg in both:
            img.give((half, "fq", sg))
    txt_grads(0, 384)
    for dz in (1, 7, 0):
        txt.give(("c", dz))
    for sg in both:
        txt.give(("z", 1, sg))
    for half in "AB":
        for sg in both:
            img.give((half, "s", 0, sg))
    for half in "AB":
        for sg in both:
            img.give((half, "f", sg))
    for sg in both:
        txt.give(("z", 0, sg))

    for side, ref, out in ((img, img_ref, img_out), (txt, txt_ref, txt_out)):
        for row in range(0, ROWS, QUARTER):
            unit, inverse = unit_of(ref[row:row + QUARTER, :])
            out[row:row + QUARTER, :] = back_norm(unit, inverse, side.total((0, 0), row, QUARTER))
    img.finish()
    txt.finish()


def on_device(image_emb, text_emb, log_temp, bias):
    rows, width = image_emb.shape
    group = 16 * rows
    n_img, n_txt = len(img_edges()), len(txt_edges())
    vmem = pl.BlockSpec(memory_space=pltpu.VMEM)
    smem = pl.BlockSpec(memory_space=pltpu.SMEM)
    return pl.pallas_call(
        kernel,
        out_shape=[jax.ShapeDtypeStruct((rows, width), jnp.float32)] * 2,
        in_specs=[vmem, vmem, smem, smem],
        out_specs=[vmem, vmem],
        scratch_shapes=(
            [pltpu.VMEM((group, width), jnp.bfloat16)] * 2
            + [pltpu.VMEM((group, group), jnp.bfloat16)]
            + [pltpu.VMEM((group, width), jnp.float32)] * 2
            + [pltpu.VMEM((group, width), jnp.bfloat16)] * 4
            + [pltpu.SemaphoreType.DMA((n_img,))] * 4
            + [pltpu.SemaphoreType.DMA((n_txt,))] * 4
        ),
        compiler_params=pltpu.CompilerParams(
            collective_id=0, has_side_effects=True, vmem_limit_bytes=56 * 2**20
        ),
    )(image_emb, text_emb, log_temp, bias)


def solution(mesh):
    placed = (P(("dp", "mp"), None), P(("dp", "mp"), None), P(), P())
    return jax.shard_map(
        on_device,
        mesh=mesh,
        in_specs=placed,
        out_specs=(P(("dp", "mp"), None), P(("dp", "mp"), None)),
        check_vma=False,
    )
```

```python
import functools

import jax
import jax.numpy as jnp
from jax import lax
from jax.experimental import pallas as pl
from jax.experimental.pallas import tpu as pltpu
from jax.sharding import PartitionSpec as P

EPS = 1e-06
MESH = pl.DeviceIdType.MESH
NX, NY, NZ = 4, 4, 8
ROWS = 64
HALF = ROWS // 2
QUARTER = ROWS // 4
NT = (((1,), (1,)), ((), ()))
TN = (((0,), (0,)), ((), ()))
NN = (((1,), (0,)), ((), ()))
CHUNKS = {1: (0, 1, 2, 3), -1: (2, 3, 0, 1)}

IMG_UNITS = (
    [((0, 0), 0), ((0, 0), 1)]
    + [((d, 0), 0) for d in (1, 3)] + [((0, d), 1) for d in (1, 3)]
    + [((0, d), 0) for d in (1, 3)] + [((d, 0), 1) for d in (1, 3)]
    + [((2, 0), 0), ((0, 2), 1)]
    + [((3, d), 0) for d in (1, 3)] + [((d, 3), 1) for d in (1, 3)]
    + [((0, 2), 0), ((2, 0), 1)]
    + [((1, d), 0) for d in (1, 3)] + [((d, 1), 1) for d in (1, 3)]
    + [((2, d), 0) for d in (1, 3)] + [((d, 2), 1) for d in (1, 3)]
    + [((3, 2), 0), ((2, 3), 1), ((1, 2), 0), ((2, 1), 1), ((2, 2), 0), ((2, 2), 1)]
)
TXT_UNITS = [((dz, s), 0) for dz in (0, 1, 7, 2, 6, 3, 5, 4) for s in (0, 1)]


class Edge:
    def __init__(self, src, dst, row, count, axis, sign):
        self.src, self.dst, self.row, self.count = src, dst, row, count
        self.axis, self.sign = axis, sign


def img_edges():
    edges = {}
    for half, first, second in (("A", "x", "y"), ("B", "y", "x")):
        base = 0 if half == "A" else HALF

        def at(df, ds, first=first):
            return (df % 4, ds % 4) if first == "x" else (ds % 4, df % 4)

        for sg in (1, -1):
            quarter = base + (0 if sg == 1 else QUARTER)
            edges[half, "f", sg] = Edge(at(0, 0), at(-sg, 0), base, HALF, first, sg)
            edges[half, "fq", sg] = Edge(at(-sg, 0), at(2, 0), quarter, QUARTER, first, sg)
            for df in range(4):
                edges[half, "s", df, sg] = Edge(at(df, 0), at(df, -sg), base, HALF, second, sg)
                edges[half, "sq", df, sg] = Edge(at(df, -sg), at(df, 2), quarter, QUARTER, second, sg)
    return edges


def txt_edges():
    edges = {}
    for sg in (1, -1):
        for k in range(4):
            for c in CHUNKS[sg][: 4 if k < 3 else 2]:
                edges["z", k, sg, c] = Edge(
                    ((-sg * k) % NZ, 0), ((-sg * (k + 1)) % NZ, 0), c * QUARTER, QUARTER, "z", sg
                )
    for dz in range(NZ):
        edges["c", dz] = Edge((dz, 0), (dz, 1), 0, ROWS, "c", 1)
    return edges


class Side:
    def __init__(self, units, edges, rows, part, out, back, sems, place):
        self.unit = 16 * ROWS // len(units)
        self.at = {unit: i * self.unit for i, unit in enumerate(units)}
        self.done = set()
        self.edges = edges
        self.number = {key: i for i, key in enumerate(edges)}
        self.rows, self.part, self.out, self.back = rows, part, out, back
        self.g_send, self.g_recv, self.r_send, self.r_recv = sems
        self.place = place
        self.sent, self.returned = set(), set()
        self.seen, self.taken = set(), set()

    def span(self, slot, row, count):
        return pl.ds(self.at[slot, row // self.unit] + row % self.unit, count)

    def gather_copy(self, key):
        e, i = self.edges[key], self.number[key]
        return pltpu.make_async_remote_copy(
            src_ref=self.rows.at[self.span(e.src, e.row, e.count)],
            dst_ref=self.rows.at[self.span(e.dst, e.row, e.count)],
            send_sem=self.g_send.at[i],
            recv_sem=self.g_recv.at[i],
            device_id=self.place(e.axis, e.sign),
            device_id_type=MESH,
        )

    def scatter_copy(self, key):
        e, i = self.edges[key], self.number[key]
        where = self.span(e.dst, e.row, e.count)
        return pltpu.make_async_remote_copy(
            src_ref=self.out.at[where],
            dst_ref=self.back.at[where],
            send_sem=self.r_send.at[i],
            recv_sem=self.r_recv.at[i],
            device_id=self.place(e.axis, -e.sign),
            device_id_type=MESH,
        )

    def send(self, *keys):
        for key in keys:
            e = self.edges[key]
            self.arrive(e.src, e.row, e.count)
            self.gather_copy(key).start()
            self.sent.add(key)

    def arrive_until(self, end):
        for (slot, which), start in self.at.items():
            if start < end:
                self.arrive(slot, which * self.unit, self.unit)

    def arrive(self, slot, row=0, count=ROWS):
        for key, e in self.edges.items():
            if e.dst == slot and e.row < row + count and row < e.row + e.count and key not in self.seen:
                assert key in self.sent, key
                self.gather_copy(key).wait_recv()
                self.seen.add(key)

    def total(self, slot, row, count):
        assert self.span(slot, row, count).start in self.done
        value = self.part[self.span(slot, row, count), :]
        for key, e in self.edges.items():
            if e.src == slot and e.row <= row and row + count <= e.row + e.count:
                if key not in self.taken:
                    assert key in self.returned, key
                    self.scatter_copy(key).wait_recv()
                    self.taken.add(key)
                value = value + self.back[self.span(e.dst, row, count), :].astype(jnp.float32)
        return value

    def give(self, *keys):
        for key in keys:
            e = self.edges[key]
            for row in range(e.row, e.row + e.count, QUARTER):
                self.out[self.span(e.dst, row, QUARTER), :] = self.total(e.dst, row, QUARTER).astype(jnp.bfloat16)
            self.scatter_copy(key).start()
            self.returned.add(key)

    def finish(self):
        assert len(self.sent) == len(self.returned) == len(self.seen) == len(self.taken) == len(self.edges)
        for key in self.edges:
            self.gather_copy(key).wait_send()
            self.scatter_copy(key).wait_send()


def unit_of(emb):
    wide = emb.astype(jnp.float32)
    inverse = lax.rsqrt(jnp.sum(wide * wide, axis=1, keepdims=True) + EPS)
    return wide * inverse, inverse


def back_norm(unit, inverse, grad):
    return inverse * (grad - unit * jnp.sum(unit * grad, axis=1, keepdims=True))


def kernel(
    img_hbm, txt_hbm, temp_hbm, bias_hbm, img_out, txt_out,
    img_ref, txt_ref, temp_ref, bias_ref, in_sems,
    p_rows, q_rows, coef, p_part, q_part, p_send, q_send, p_back, q_back,
    pg_send, pg_recv, pr_send, pr_recv, qg_send, qg_recv, qr_send, qr_recv,
):
    loads = [
        pltpu.make_async_copy(here, there, in_sems.at[i])
        for i, (here, there) in enumerate(
            ((img_hbm, img_ref), (txt_hbm, txt_ref), (temp_hbm, temp_ref), (bias_hbm, bias_ref))
        )
    ]
    for load in loads:
        load.start()
    dp, mp = lax.axis_index("dp"), lax.axis_index("mp")
    core, z, x = dp % 2, (dp // 2) % NZ, (dp // (2 * NZ)) * 2 + mp // NY
    y = mp % NY

    def place(axis, sign):
        nx, ny, nz, nc = x, y, z, core
        if axis == "x":
            nx = (x + sign + NX) % NX
        elif axis == "y":
            ny = (y + sign + NY) % NY
        elif axis == "z":
            nz = (z + sign + NZ) % NZ
        else:
            nc = 1 - core
        return ((nx // 2) * (2 * NZ) + nz * 2 + nc, (nx % 2) * NY + ny)

    barrier = pltpu.get_barrier_semaphore()
    neighbours = [place(a, s) for a in "xyz" for s in (1, -1)] + [place("c", 1)]
    for device in neighbours:
        pl.semaphore_signal(barrier, inc=1, device_id=device, device_id_type=MESH)

    img = Side(IMG_UNITS, img_edges(), p_rows, p_part, p_send, p_back,
               (pg_send, pg_recv, pr_send, pr_recv), place)
    txt = Side(TXT_UNITS, txt_edges(), q_rows, q_part, q_send, q_back,
               (qg_send, qg_recv, qr_send, qr_recv), place)

    for load in loads:
        load.wait()
    half_tau = 0.5 * jnp.exp(temp_ref[...].reshape(1, 1))
    half_bias = 0.5 * bias_ref[...].reshape(1, 1)

    p_rows[0:ROWS, :] = unit_of(img_ref[...])[0].astype(jnp.bfloat16)
    q_rows[0:ROWS, :] = unit_of(txt_ref[...])[0].astype(jnp.bfloat16)
    pl.semaphore_wait(barrier, len(neighbours))

    def scores(t0, tn, i0, n):
        txt.arrive_until(t0 + tn)
        img.arrive_until(i0 + n)
        dots = lax.dot_general(q_rows[t0:t0 + tn, :], p_rows[i0:i0 + n, :], NT,
                               preferred_element_type=jnp.float32)
        wave = jnp.tanh(half_tau * dots + half_bias)
        coef[t0:t0 + tn, i0:i0 + n] = (half_tau * wave + half_tau).astype(jnp.bfloat16)

    def own_scores():
        dots = lax.dot_general(q_rows[0:ROWS, :], p_rows[0:128, :], NT,
                               preferred_element_type=jnp.float32)
        wave = jnp.tanh(half_tau * dots + half_bias)
        same = lax.broadcasted_iota(jnp.int32, dots.shape, 0) == lax.broadcasted_iota(jnp.int32, dots.shape, 1)
        coef[0:ROWS, 0:128] = (half_tau * wave + jnp.where(same, -half_tau, half_tau)).astype(jnp.bfloat16)

    def img_grads(i0, n):
        img.done.update(range(i0, i0 + n, QUARTER))
        p_part[i0:i0 + n, :] = lax.dot_general(coef[:, i0:i0 + n], q_rows[...], TN,
                                               preferred_element_type=jnp.float32)

    def txt_grads(t0, n):
        txt.done.update(range(t0, t0 + n, QUARTER))
        q_part[t0:t0 + n, :] = lax.dot_general(coef[t0:t0 + n, :], p_rows[...], NN,
                                               preferred_element_type=jnp.float32)

    both = (1, -1)

    def ring(k, *places):
        for i in places:
            for sg in both:
                txt.send(("z", k, sg, CHUNKS[sg][i]))

    def ring_back(k, *places):
        for i in places:
            for sg in both:
                txt.give(("z", k, sg, CHUNKS[sg][i]))

    def across(kind, *far, way=img.send):
        for df in far:
            for half in "AB":
                for sg in both:
                    way((half, kind, df, sg))

    def along(kind, way=img.send):
        for half in "AB":
            for sg in both:
                way((half, kind, sg))

    along("f")
    ring(0, 0, 1, 2, 3)
    across("s", 0)
    txt.send(("c", 0))
    ring(1, 0)
    along("fq")
    across("s", 3)
    ring(1, 1, 2)
    across("sq", 0)
    ring(1, 3)
    txt.send(("c", 1), ("c", 7))
    across("s", 1)
    ring(2, 0)
    across("s", 2)
    ring(2, 1)
    scores(0, 384, 0, 384)
    own_scores()
    ring(2, 2)
    across("sq", 3)
    ring(2, 3)
    txt.send(("c", 2), ("c", 6))
    ring(3, 0)
    scores(384, 256, 0, 384)
    ring(3, 1)
    across("sq", 1)
    scores(0, 640, 384, 256)
    txt.send(("c", 3), ("c", 5))
    across("sq", 2)
    txt.send(("c", 4))
    scores(640, 256, 0, 640)
    scores(0, 896, 640, 256)
    scores(0, 896, 896, 128)
    scores(896, 128, 0, 1024)

    txt_grads(896, 128)
    txt.give(("c", 4))
    img_grads(768, 256)
    across("sq", 2, 3, 1, way=img.give)
    txt_grads(640, 256)
    txt.give(("c", 3), ("c", 5))
    ring_back(3, 0, 1)
    img_grads(512, 256)
    across("sq", 0, way=img.give)
    ring_back(2, 2, 3)
    across("s", 2, way=img.give)
    txt_grads(384, 256)
    txt.give(("c", 2), ("c", 6))
    ring_back(2, 0, 1)
    img_grads(256, 256)
    across("s", 3, 1, way=img.give)
    ring_back(1, 2, 3)
    txt_grads(0, 384)
    txt.give(("c", 1), ("c", 7), ("c", 0))
    ring_back(1, 0, 1)
    img_grads(0, 256)
    along("fq", way=img.give)
    across("s", 0, way=img.give)
    ring_back(0, 2, 3, 0, 1)
    along("f", way=img.give)

    for side, ref, out in ((img, img_ref, img_out), (txt, txt_ref, txt_out)):
        for row in range(0, ROWS, QUARTER):
            unit, inverse = unit_of(ref[row:row + QUARTER, :])
            out[row:row + QUARTER, :] = back_norm(unit, inverse, side.total((0, 0), row, QUARTER))
    img.finish()
    txt.finish()


def on_device(image_emb, text_emb, log_temp, bias):
    rows, width = image_emb.shape
    group = 16 * rows
    n_img, n_txt = len(img_edges()), len(txt_edges())
    vmem = pl.BlockSpec(memory_space=pltpu.VMEM)
    hbm = pl.BlockSpec(memory_space=pltpu.HBM)
    return pl.pallas_call(
        kernel,
        out_shape=[pltpu.VMEM((rows, width), jnp.float32)] * 2,
        in_specs=[pl.BlockSpec(memory_space=pl.ANY)] * 4,
        out_specs=[vmem, vmem],
        scratch_shapes=(
            [pltpu.VMEM((rows, width), jnp.bfloat16)] * 2
            + [pltpu.VMEM((1,), jnp.float32)] * 2
            + [pltpu.SemaphoreType.DMA((4,))]
            + [pltpu.VMEM((group, width), jnp.bfloat16)] * 2
            + [pltpu.VMEM((group, group), jnp.bfloat16)]
            + [pltpu.VMEM((group, width), jnp.float32)] * 2
            + [pltpu.VMEM((group, width), jnp.bfloat16)] * 4
            + [pltpu.SemaphoreType.DMA((n_img,))] * 4
            + [pltpu.SemaphoreType.DMA((n_txt,))] * 4
        ),
        compiler_params=pltpu.CompilerParams(
            collective_id=0, has_side_effects=True, vmem_limit_bytes=56 * 2**20
        ),
    )(image_emb, text_emb, log_temp, bias)


def solution(mesh):
    placed = (P(("dp", "mp"), None), P(("dp", "mp"), None), P(), P())
    return jax.shard_map(
        on_device,
        mesh=mesh,
        in_specs=placed,
        out_specs=(P(("dp", "mp"), None), P(("dp", "mp"), None)),
        check_vma=False,
    )
```

```python
import functools

import jax
import jax.numpy as jnp
from jax import lax
from jax.experimental import pallas as pl
from jax.experimental.pallas import tpu as pltpu
from jax.sharding import PartitionSpec as P

EPS = 1e-06
MESH = pl.DeviceIdType.MESH
NX, NY, NZ = 4, 4, 8
ROWS = 64
HALF = ROWS // 2
QUARTER = ROWS // 4
NT = (((1,), (1,)), ((), ()))
TN = (((0,), (0,)), ((), ()))
NN = (((1,), (0,)), ((), ()))
CHUNKS = {1: (0, 1, 2, 3), -1: (2, 3, 0, 1)}

IMG_UNITS = (
    [((0, 0), 0), ((0, 0), 1)]
    + [((d, 0), 0) for d in (1, 3)] + [((0, d), 1) for d in (1, 3)]
    + [((0, d), 0) for d in (1, 3)] + [((d, 0), 1) for d in (1, 3)]
    + [((2, 0), 0), ((0, 2), 1)]
    + [((3, d), 0) for d in (1, 3)] + [((d, 3), 1) for d in (1, 3)]
    + [((1, d), 0) for d in (1, 3)] + [((d, 1), 1) for d in (1, 3)]
    + [((2, d), 0) for d in (1, 3)] + [((d, 2), 1) for d in (1, 3)]
    + [((0, 2), 0), ((2, 0), 1)]
    + [((3, 2), 0), ((2, 3), 1), ((1, 2), 0), ((2, 1), 1), ((2, 2), 0), ((2, 2), 1)]
)
TXT_UNITS = [((dz, s), 0) for dz in (0, 1, 7, 2, 6, 3, 5, 4) for s in (0, 1)]


PLAN = (
    ("send", "t", "z", 0, 1, 0), ("send", "t", "z", 0, -1, 2), ("send", "i", "f", "A", 0, 1, 0),
    ("send", "i", "f", "A", 0, -1, 0), ("send", "t", "z", 0, 1, 1), ("send", "i", "f", "B", 0, -1, 0),
    ("send", "t", "z", 0, 1, 2), ("send", "i", "f", "B", 0, 1, 0), ("send", "i", "f", "A", 0, -1, 1),
    ("send", "i", "f", "B", 0, 1, 1), ("send", "i", "s", "A", 0, -1, 0), ("send", "i", "s", "B", 0, 1, 1),
    ("send", "t", "z", 0, 1, 3), ("send", "t", "z", 0, -1, 3), ("send", "i", "f", "A", 0, 1, 1),
    ("send", "i", "s", "B", 0, -1, 0), ("send", "i", "s", "B", 0, -1, 1), ("send", "t", "z", 0, -1, 0),
    ("send", "i", "s", "A", 0, 1, 0), ("send", "i", "s", "B", 0, 1, 0), ("send", "i", "s", "A", 0, -1, 1),
    ("send", "t", "z", 0, -1, 1), ("send", "i", "f", "B", 0, -1, 1), ("send", "t", "c", 0, 1),
    ("send", "i", "s", "A", 0, 1, 1), ("send", "t", "c", 0, 0), ("send", "t", "z", 1, 1, 0),
    ("send", "t", "z", 1, -1, 2), ("send", "i", "fq", "A", 0, 1, 0), ("send", "i", "fq", "A", 0, -1, 0),
    ("send", "i", "fq", "B", 0, -1, 0), ("send", "i", "fq", "B", 0, 1, 0), ("send", "t", "z", 1, 1, 1),
    ("send", "t", "z", 1, -1, 3), ("send", "i", "s", "B", 1, 1, 1), ("send", "i", "s", "A", 3, -1, 1),
    ("send", "i", "s", "B", 3, -1, 1), ("send", "t", "c", 1, 1), ("send", "i", "s", "A", 3, 1, 0),
    ("send", "t", "z", 1, -1, 0), ("send", "i", "s", "B", 3, 1, 0), ("send", "i", "s", "B", 3, -1, 0),
    ("send", "t", "z", 1, 1, 2), ("send", "i", "s", "A", 3, -1, 0), ("send", "i", "s", "A", 3, 1, 1),
    ("send", "i", "s", "B", 3, 1, 1), ("send", "i", "sq", "B", 0, -1, 0), ("send", "t", "z", 1, -1, 1),
    ("send", "t", "z", 1, 1, 3), ("send", "i", "s", "B", 1, -1, 0), ("send", "i", "s", "B", 1, 1, 0),
    ("send", "i", "s", "A", 1, -1, 0), ("send", "i", "s", "A", 1, 1, 0), ("send", "i", "sq", "A", 0, -1, 0),
    ("send", "i", "sq", "A", 0, 1, 0), ("send", "t", "z", 2, 1, 0), ("send", "t", "z", 2, -1, 2),
    ("send", "t", "c", 1, 0), ("send", "i", "s", "A", 2, 1, 0), ("send", "i", "s", "A", 2, -1, 0),
    ("send", "i", "s", "A", 1, 1, 1), ("send", "i", "s", "B", 2, -1, 0), ("send", "i", "s", "B", 2, 1, 0),
    ("send", "t", "z", 2, 1, 1), ("send", "t", "z", 2, -1, 3), ("send", "i", "s", "A", 1, -1, 1),
    ("send", "i", "s", "A", 2, -1, 1), ("send", "t", "c", 7, 0), ("send", "i", "s", "B", 1, -1, 1),
    ("send", "i", "s", "B", 2, 1, 1), ("send", "t", "c", 2, 1), ("send", "t", "c", 6, 0),
    ("send", "t", "z", 2, -1, 0), ("send", "i", "s", "A", 2, 1, 1), ("send", "i", "sq", "B", 3, -1, 0),
    ("send", "i", "sq", "B", 3, 1, 0), ("send", "t", "c", 7, 1), ("send", "t", "z", 2, 1, 2),
    ("send", "i", "s", "B", 2, -1, 1), ("send", "t", "z", 2, -1, 1), ("send", "i", "sq", "A", 3, 1, 0),
    ("send", "i", "sq", "A", 3, -1, 0), ("send", "t", "z", 2, 1, 3), ("send", "i", "sq", "B", 0, 1, 0),
    ("send", "t", "c", 2, 0), ("send", "i", "sq", "A", 1, -1, 0), ("send", "t", "c", 6, 1),
    ("send", "t", "z", 3, 1, 0), ("send", "t", "z", 3, -1, 2), ("send", "i", "sq", "A", 1, 1, 0),
    ("send", "i", "sq", "B", 1, 1, 0), ("send", "i", "sq", "B", 1, -1, 0), ("coef", 0, 384, 0, 384), ("own",),
    ("send", "t", "z", 3, 1, 1), ("send", "t", "z", 3, -1, 3), ("send", "i", "sq", "A", 2, -1, 0),
    ("send", "i", "sq", "B", 2, 1, 0), ("send", "t", "c", 5, 0), ("send", "i", "sq", "A", 2, 1, 0),
    ("send", "i", "sq", "B", 2, -1, 0), ("send", "t", "c", 3, 1), ("coef", 384, 256, 0, 640),
    ("coef", 0, 384, 384, 256), ("send", "t", "c", 3, 0), ("send", "t", "c", 5, 1), ("coef", 0, 640, 640, 256),
    ("coef", 640, 256, 0, 896), ("send", "t", "c", 4, 0), ("send", "t", "c", 4, 1), ("coef", 0, 896, 896, 128),
    ("coef", 896, 128, 0, 1024), ("txt", 896, 128, 0, 1024), ("give", "t", "c", 4, 1), ("give", "t", "c", 4, 0),
    ("img", 896, 128, 0, 1024), ("give", "i", "sq", "A", 2, 1, 0), ("give", "i", "sq", "B", 2, -1, 0),
    ("give", "i", "sq", "B", 2, 1, 0), ("give", "i", "sq", "A", 2, -1, 0), ("txt", 640, 256, 0, 1024),
    ("give", "t", "z", 3, -1, 2), ("give", "t", "z", 3, 1, 0), ("give", "t", "z", 3, 1, 1),
    ("give", "i", "sq", "A", 1, 1, 0), ("img", 768, 128, 0, 1024), ("give", "i", "sq", "A", 1, -1, 0),
    ("give", "i", "sq", "B", 3, -1, 0), ("give", "i", "sq", "B", 1, 1, 0), ("give", "i", "sq", "B", 3, 1, 0),
    ("give", "t", "c", 3, 0), ("give", "t", "c", 5, 1), ("give", "t", "c", 5, 0), ("give", "i", "sq", "A", 3, -1, 0),
    ("give", "t", "z", 3, -1, 3), ("give", "i", "sq", "B", 1, -1, 0), ("give", "i", "sq", "B", 0, 1, 0),
    ("give", "i", "sq", "A", 3, 1, 0), ("img", 512, 256, 0, 1024), ("give", "t", "z", 2, -1, 0),
    ("give", "t", "z", 2, 1, 2), ("give", "i", "sq", "B", 0, -1, 0), ("give", "i", "s", "B", 2, -1, 1),
    ("give", "t", "z", 2, 1, 3), ("give", "t", "c", 3, 1), ("give", "t", "z", 2, -1, 1),
    ("give", "i", "s", "A", 2, 1, 1), ("give", "i", "sq", "A", 0, 1, 0), ("give", "i", "s", "B", 2, 1, 1),
    ("give", "i", "s", "A", 2, -1, 1), ("txt", 384, 256, 0, 1024), ("give", "i", "s", "A", 2, 1, 0),
    ("give", "i", "s", "A", 1, -1, 1), ("give", "i", "s", "B", 2, -1, 0), ("give", "t", "c", 2, 0),
    ("give", "i", "s", "B", 2, 1, 0), ("give", "i", "s", "A", 1, 1, 1), ("give", "i", "s", "A", 2, -1, 0),
    ("give", "i", "sq", "A", 0, -1, 0), ("give", "t", "z", 2, -1, 2), ("give", "t", "z", 2, 1, 0),
    ("img", 256, 256, 0, 1024), ("give", "t", "z", 2, 1, 1), ("give", "t", "z", 2, -1, 3), ("give", "t", "c", 6, 1),
    ("give", "i", "s", "A", 1, -1, 0), ("give", "i", "s", "A", 3, 1, 0), ("give", "i", "s", "B", 1, 1, 1),
    ("give", "i", "s", "B", 1, 1, 0), ("give", "i", "s", "B", 1, -1, 1), ("give", "i", "s", "B", 3, -1, 0),
    ("txt", 128, 256, 0, 1024), ("give", "t", "z", 1, 1, 2), ("give", "t", "z", 1, -1, 0), ("give", "t", "c", 6, 0),
    ("give", "i", "s", "B", 3, 1, 1), ("give", "i", "s", "A", 3, -1, 0), ("give", "i", "s", "B", 1, -1, 0),
    ("give", "i", "s", "B", 3, 1, 0), ("give", "i", "s", "A", 3, -1, 1), ("give", "i", "s", "A", 3, 1, 1),
    ("give", "i", "s", "B", 3, -1, 1), ("give", "t", "c", 7, 0), ("give", "i", "s", "A", 1, 1, 0),
    ("give", "t", "c", 7, 1), ("give", "t", "c", 2, 1), ("give", "t", "z", 1, 1, 3), ("give", "t", "z", 1, -1, 1),
    ("img", 0, 256, 0, 1024), ("give", "t", "z", 1, 1, 0), ("give", "t", "z", 1, -1, 2),
    ("give", "i", "fq", "B", 0, -1, 0), ("give", "i", "fq", "A", 0, -1, 0), ("give", "i", "fq", "A", 0, 1, 0),
    ("give", "t", "c", 1, 1), ("give", "i", "fq", "B", 0, 1, 0), ("give", "i", "s", "B", 0, -1, 1),
    ("give", "i", "s", "A", 0, -1, 1), ("give", "i", "s", "A", 0, 1, 1), ("give", "i", "s", "B", 0, 1, 0),
    ("give", "t", "z", 1, 1, 1), ("give", "t", "z", 1, -1, 3), ("give", "i", "s", "B", 0, -1, 0),
    ("give", "t", "c", 1, 0), ("give", "i", "s", "B", 0, 1, 1), ("txt", 0, 128, 0, 1024),
    ("give", "i", "s", "A", 0, 1, 0), ("give", "t", "z", 0, 1, 2), ("give", "t", "z", 0, -1, 0),
    ("give", "i", "f", "B", 0, -1, 1), ("give", "t", "z", 0, 1, 3), ("give", "t", "z", 0, -1, 1),
    ("give", "t", "c", 0, 0), ("give", "t", "c", 0, 1), ("give", "i", "f", "A", 0, 1, 1),
    ("give", "i", "f", "B", 0, 1, 1), ("give", "i", "f", "A", 0, -1, 1), ("give", "i", "s", "A", 0, -1, 0),
    ("give", "t", "z", 0, 1, 0), ("give", "t", "z", 0, -1, 2), ("give", "i", "f", "B", 0, -1, 0),
    ("give", "i", "f", "B", 0, 1, 0), ("give", "i", "f", "A", 0, 1, 0), ("give", "i", "f", "A", 0, -1, 0),
    ("give", "t", "z", 0, 1, 1), ("give", "t", "z", 0, -1, 3),
)

class Edge:
    def __init__(self, src, dst, row, count, axis, sign):
        self.src, self.dst, self.row, self.count = src, dst, row, count
        self.axis, self.sign = axis, sign


def img_edges():
    edges = {}
    for half, first, second in (("A", "x", "y"), ("B", "y", "x")):
        base = 0 if half == "A" else HALF

        def at(df, ds, first=first):
            return (df % 4, ds % 4) if first == "x" else (ds % 4, df % 4)

        for sg in (1, -1):
            rows = (base, base + QUARTER) if sg == 1 else (base + QUARTER, base)
            for i in (0, 1):
                edges["f", half, 0, sg, i] = Edge(at(0, 0), at(-sg, 0), rows[i], QUARTER, first, sg)
            edges["fq", half, 0, sg, 0] = Edge(at(-sg, 0), at(2, 0), rows[0], QUARTER, first, sg)
            for df in range(4):
                for i in (0, 1):
                    edges["s", half, df, sg, i] = Edge(at(df, 0), at(df, -sg), rows[i], QUARTER, second, sg)
                edges["sq", half, df, sg, 0] = Edge(at(df, -sg), at(df, 2), rows[0], QUARTER, second, sg)
    return edges


def txt_edges():
    edges = {}
    for sg in (1, -1):
        for k in range(4):
            for c in CHUNKS[sg][: 4 if k < 3 else 2]:
                edges["z", k, sg, c] = Edge(
                    ((-sg * k) % NZ, 0), ((-sg * (k + 1)) % NZ, 0), c * QUARTER, QUARTER, "z", sg
                )
    for dz in range(NZ):
        for h in (0, 1):
            edges["c", dz, h] = Edge((dz, 0), (dz, 1), h * HALF, HALF, "c", 1)
    return edges


class Side:
    def __init__(self, units, edges, rows, part, out, back, sems, place):
        self.unit = 16 * ROWS // len(units)
        self.at = {unit: i * self.unit for i, unit in enumerate(units)}
        self.done = {}
        self.edges = edges
        self.number = {key: i for i, key in enumerate(edges)}
        self.rows, self.part, self.out, self.back = rows, part, out, back
        self.g_send, self.g_recv, self.r_send, self.r_recv = sems
        self.place = place
        self.sent, self.returned = set(), set()
        self.seen, self.taken = set(), set()

    def span(self, slot, row, count):
        return pl.ds(self.at[slot, row // self.unit] + row % self.unit, count)

    def gather_copy(self, key):
        e, i = self.edges[key], self.number[key]
        return pltpu.make_async_remote_copy(
            src_ref=self.rows.at[self.span(e.src, e.row, e.count)],
            dst_ref=self.rows.at[self.span(e.dst, e.row, e.count)],
            send_sem=self.g_send.at[i],
            recv_sem=self.g_recv.at[i],
            device_id=self.place(e.axis, e.sign),
            device_id_type=MESH,
        )

    def scatter_copy(self, key):
        e, i = self.edges[key], self.number[key]
        where = self.span(e.dst, e.row, e.count)
        return pltpu.make_async_remote_copy(
            src_ref=self.out.at[where],
            dst_ref=self.back.at[where],
            send_sem=self.r_send.at[i],
            recv_sem=self.r_recv.at[i],
            device_id=self.place(e.axis, -e.sign),
            device_id_type=MESH,
        )

    def send(self, *keys):
        for key in keys:
            e = self.edges[key]
            self.arrive(e.src, e.row, e.count)
            self.gather_copy(key).start()
            self.sent.add(key)

    def arrive_until(self, end):
        for (slot, which), start in self.at.items():
            if start < end:
                self.arrive(slot, which * self.unit, self.unit)

    def arrive(self, slot, row=0, count=ROWS):
        for key, e in self.edges.items():
            if e.dst == slot and e.row < row + count and row < e.row + e.count and key not in self.seen:
                assert key in self.sent, key
                self.gather_copy(key).wait_recv()
                self.seen.add(key)

    def total(self, slot, row, count):
        assert self.done[self.span(slot, row, count).start] == 16 * ROWS
        value = self.part[self.span(slot, row, count), :]
        for key, e in self.edges.items():
            if e.src == slot and e.row <= row and row + count <= e.row + e.count:
                if key not in self.taken:
                    assert key in self.returned, key
                    self.scatter_copy(key).wait_recv()
                    self.taken.add(key)
                value = value + self.back[self.span(e.dst, row, count), :].astype(jnp.float32)
        return value

    def add(self, part, start, count, first, length):
        had = {self.done.get(row, 0) for row in range(start, start + count, QUARTER)}
        assert len(had) == 1
        had = had.pop()
        for row in range(start, start + count, QUARTER):
            self.done[row] = had + length
        return part if had == 0 else self.part[start:start + count, :] + part

    def give(self, *keys):
        for key in keys:
            e = self.edges[key]
            for row in range(e.row, e.row + e.count, QUARTER):
                self.out[self.span(e.dst, row, QUARTER), :] = self.total(e.dst, row, QUARTER).astype(jnp.bfloat16)
            self.scatter_copy(key).start()
            self.returned.add(key)

    def finish(self):
        assert len(self.sent) == len(self.returned) == len(self.seen) == len(self.taken) == len(self.edges)
        for key in self.edges:
            self.gather_copy(key).wait_send()
            self.scatter_copy(key).wait_send()


def unit_of(emb):
    wide = emb.astype(jnp.float32)
    inverse = lax.rsqrt(jnp.sum(wide * wide, axis=1, keepdims=True) + EPS)
    return wide * inverse, inverse


def back_norm(unit, inverse, grad):
    return inverse * (grad - unit * jnp.sum(unit * grad, axis=1, keepdims=True))


def kernel(
    img_hbm, txt_hbm, temp_hbm, bias_hbm, img_out, txt_out,
    img_ref, txt_ref, temp_ref, bias_ref, in_sems,
    p_rows, q_rows, coef, p_part, q_part, p_send, q_send, p_back, q_back,
    pg_send, pg_recv, pr_send, pr_recv, qg_send, qg_recv, qr_send, qr_recv,
):
    loads = [
        pltpu.make_async_copy(here, there, in_sems.at[i])
        for i, (here, there) in enumerate(
            ((img_hbm, img_ref), (txt_hbm, txt_ref), (temp_hbm, temp_ref), (bias_hbm, bias_ref))
        )
    ]
    for load in loads:
        load.start()
    dp, mp = lax.axis_index("dp"), lax.axis_index("mp")
    core, z, x = dp % 2, (dp // 2) % NZ, (dp // (2 * NZ)) * 2 + mp // NY
    y = mp % NY

    def place(axis, sign):
        nx, ny, nz, nc = x, y, z, core
        if axis == "x":
            nx = (x + sign + NX) % NX
        elif axis == "y":
            ny = (y + sign + NY) % NY
        elif axis == "z":
            nz = (z + sign + NZ) % NZ
        else:
            nc = 1 - core
        return ((nx // 2) * (2 * NZ) + nz * 2 + nc, (nx % 2) * NY + ny)

    barrier = pltpu.get_barrier_semaphore()
    neighbours = [place(a, s) for a in "xyz" for s in (1, -1)] + [place("c", 1)]
    for device in neighbours:
        pl.semaphore_signal(barrier, inc=1, device_id=device, device_id_type=MESH)

    img = Side(IMG_UNITS, img_edges(), p_rows, p_part, p_send, p_back,
               (pg_send, pg_recv, pr_send, pr_recv), place)
    txt = Side(TXT_UNITS, txt_edges(), q_rows, q_part, q_send, q_back,
               (qg_send, qg_recv, qr_send, qr_recv), place)

    for load in loads:
        load.wait()
    half_tau = 0.5 * jnp.exp(temp_ref[...].reshape(1, 1))
    half_bias = 0.5 * bias_ref[...].reshape(1, 1)

    p_rows[0:ROWS, :] = unit_of(img_ref[...])[0].astype(jnp.bfloat16)
    q_rows[0:ROWS, :] = unit_of(txt_ref[...])[0].astype(jnp.bfloat16)
    pl.semaphore_wait(barrier, len(neighbours))

    def scores(t0, tn, i0, n):
        txt.arrive_until(t0 + tn)
        img.arrive_until(i0 + n)
        dots = lax.dot_general(q_rows[t0:t0 + tn, :], p_rows[i0:i0 + n, :], NT,
                               preferred_element_type=jnp.float32)
        wave = jnp.tanh(half_tau * dots + half_bias)
        coef[t0:t0 + tn, i0:i0 + n] = (half_tau * wave + half_tau).astype(jnp.bfloat16)

    def own_scores():
        dots = lax.dot_general(q_rows[0:ROWS, :], p_rows[0:128, :], NT,
                               preferred_element_type=jnp.float32)
        wave = jnp.tanh(half_tau * dots + half_bias)
        same = lax.broadcasted_iota(jnp.int32, dots.shape, 0) == lax.broadcasted_iota(jnp.int32, dots.shape, 1)
        coef[0:ROWS, 0:128] = (half_tau * wave + jnp.where(same, -half_tau, half_tau)).astype(jnp.bfloat16)

    def img_grads(i0, n, t0, tn):
        part = lax.dot_general(coef[t0:t0 + tn, i0:i0 + n], q_rows[t0:t0 + tn, :], TN,
                               preferred_element_type=jnp.float32)
        p_part[i0:i0 + n, :] = img.add(part, i0, n, t0, tn)

    def txt_grads(t0, n, i0, tn):
        part = lax.dot_general(coef[t0:t0 + n, i0:i0 + tn], p_rows[i0:i0 + tn, :], NN,
                               preferred_element_type=jnp.float32)
        q_part[t0:t0 + n, :] = txt.add(part, t0, n, i0, tn)

    sides = {"i": img, "t": txt}
    for step in PLAN:
        if step[0] == "send":
            sides[step[1]].send(step[2:])
        elif step[0] == "give":
            sides[step[1]].give(step[2:])
        elif step[0] == "coef":
            scores(*step[1:])
        elif step[0] == "own":
            assert ("coef", 0, 384, 0, 384) in PLAN[: PLAN.index(step)]
            own_scores()
        elif step[0] == "img":
            img_grads(*step[1:])
        else:
            txt_grads(*step[1:])

    for side, ref, out in ((img, img_ref, img_out), (txt, txt_ref, txt_out)):
        for row in range(0, ROWS, QUARTER):
            unit, inverse = unit_of(ref[row:row + QUARTER, :])
            out[row:row + QUARTER, :] = back_norm(unit, inverse, side.total((0, 0), row, QUARTER))
    img.finish()
    txt.finish()


def store_kernel(img_ref, txt_ref, img_out, txt_out, sems):
    stores = [
        pltpu.make_async_copy(here, there, sems.at[i])
        for i, (here, there) in enumerate(((img_ref, img_out), (txt_ref, txt_out)))
    ]
    for store in stores:
        store.start()
    for store in stores:
        store.wait()


def on_device(image_emb, text_emb, log_temp, bias):
    rows, width = image_emb.shape
    group = 16 * rows
    n_img, n_txt = len(img_edges()), len(txt_edges())
    vmem = pl.BlockSpec(memory_space=pltpu.VMEM)
    hbm = pl.BlockSpec(memory_space=pltpu.HBM)
    grads = pl.pallas_call(
        kernel,
        out_shape=[pltpu.VMEM((rows, width), jnp.float32)] * 2,
        in_specs=[pl.BlockSpec(memory_space=pl.ANY)] * 4,
        out_specs=[vmem, vmem],
        scratch_shapes=(
            [pltpu.VMEM((rows, width), jnp.bfloat16)] * 2
            + [pltpu.VMEM((1,), jnp.float32)] * 2
            + [pltpu.SemaphoreType.DMA((4,))]
            + [pltpu.VMEM((group, width), jnp.bfloat16)] * 2
            + [pltpu.VMEM((group, group), jnp.bfloat16)]
            + [pltpu.VMEM((group, width), jnp.float32)] * 2
            + [pltpu.VMEM((group, width), jnp.bfloat16)] * 4
            + [pltpu.SemaphoreType.DMA((n_img,))] * 4
            + [pltpu.SemaphoreType.DMA((n_txt,))] * 4
        ),
        compiler_params=pltpu.CompilerParams(
            collective_id=0, has_side_effects=True, vmem_limit_bytes=56 * 2**20
        ),
    )(image_emb, text_emb, log_temp, bias)
    anywhere = pl.BlockSpec(memory_space=pl.ANY)
    return pl.pallas_call(
        store_kernel,
        out_shape=[jax.ShapeDtypeStruct((rows, width), jnp.float32)] * 2,
        in_specs=[vmem] * 2,
        out_specs=[anywhere] * 2,
        scratch_shapes=[pltpu.SemaphoreType.DMA((2,))],
    )(*(pltpu.with_memory_space_constraint(grad, pltpu.VMEM) for grad in grads))


def solution(mesh):
    placed = (P(("dp", "mp"), None), P(("dp", "mp"), None), P(), P())
    return jax.shard_map(
        on_device,
        mesh=mesh,
        in_specs=placed,
        out_specs=(P(("dp", "mp"), None), P(("dp", "mp"), None)),
        check_vma=False,
    )
```

```python
import functools

import jax
import jax.numpy as jnp
from jax import lax
from jax.experimental import pallas as pl
from jax.experimental.pallas import tpu as pltpu
from jax.sharding import PartitionSpec as P

EPS = 1e-06
MESH = pl.DeviceIdType.MESH
NX, NY, NZ = 4, 4, 8
ROWS = 64
HALF = ROWS // 2
QUARTER = ROWS // 4
NT = (((1,), (1,)), ((), ()))
TN = (((0,), (0,)), ((), ()))
NN = (((1,), (0,)), ((), ()))
CHUNKS = {1: (0, 1, 2, 3), -1: (2, 3, 0, 1)}

IMG_UNITS = (
    [((0, 0), 0), ((0, 0), 1)]
    + [((d, 0), 0) for d in (1, 3)] + [((0, d), 1) for d in (1, 3)]
    + [((0, d), 0) for d in (1, 3)] + [((d, 0), 1) for d in (1, 3)]
    + [((2, 0), 0), ((0, 2), 1)]
    + [((3, d), 0) for d in (1, 3)] + [((d, 3), 1) for d in (1, 3)]
    + [((1, d), 0) for d in (1, 3)] + [((d, 1), 1) for d in (1, 3)]
    + [((2, d), 0) for d in (1, 3)] + [((d, 2), 1) for d in (1, 3)]
    + [((0, 2), 0), ((2, 0), 1)]
    + [((3, 2), 0), ((2, 3), 1), ((1, 2), 0), ((2, 1), 1), ((2, 2), 0), ((2, 2), 1)]
)
TXT_UNITS = [((dz, s), 0) for dz in (0, 1, 7, 2, 6, 3, 5, 4) for s in (0, 1)]


PLAN = (
    ("send", "t", "z", 0, -1, 2), ("send", "t", "z", 0, 1, 0), ("send", "t", "z", 0, -1, 3),
    ("send", "i", "f", "A", 0, 1, 0), ("send", "i", "f", "B", 0, -1, 0), ("send", "t", "z", 0, 1, 1),
    ("send", "i", "f", "B", 0, 1, 0), ("send", "i", "f", "A", 0, -1, 0), ("send", "t", "z", 0, -1, 0),
    ("send", "i", "f", "A", 0, 1, 1), ("send", "t", "z", 0, 1, 3), ("send", "i", "s", "A", 0, -1, 0),
    ("send", "i", "s", "B", 0, -1, 1), ("send", "t", "z", 0, 1, 2), ("send", "i", "f", "B", 0, -1, 1),
    ("send", "i", "s", "B", 0, 1, 0), ("send", "i", "s", "A", 0, 1, 1), ("send", "i", "f", "B", 0, 1, 1),
    ("send", "i", "s", "A", 0, 1, 0), ("send", "i", "s", "B", 0, 1, 1), ("send", "i", "f", "A", 0, -1, 1),
    ("send", "i", "s", "B", 0, -1, 0), ("send", "i", "s", "A", 0, -1, 1), ("send", "t", "z", 0, -1, 1),
    ("send", "t", "z", 1, -1, 2), ("send", "t", "z", 1, 1, 0), ("send", "i", "fq", "A", 0, 1, 0),
    ("send", "i", "fq", "B", 0, -1, 0), ("send", "i", "s", "A", 1, -1, 0), ("send", "i", "fq", "A", 0, -1, 0),
    ("send", "i", "fq", "B", 0, 1, 0), ("send", "i", "s", "B", 1, 1, 1), ("send", "i", "s", "B", 3, -1, 1),
    ("send", "t", "z", 1, -1, 3), ("send", "t", "z", 1, 1, 1), ("send", "i", "s", "B", 3, 1, 0),
    ("send", "i", "sq", "A", 0, -1, 0), ("send", "i", "s", "B", 1, -1, 0), ("send", "i", "s", "A", 3, 1, 0),
    ("send", "t", "z", 1, -1, 0), ("send", "i", "sq", "B", 0, 1, 0), ("send", "t", "c", 1, 1),
    ("send", "t", "z", 1, 1, 3), ("send", "t", "c", 7, 0), ("send", "i", "s", "B", 3, -1, 0),
    ("send", "i", "s", "B", 3, 1, 1), ("send", "i", "s", "A", 1, 1, 1), ("send", "i", "s", "A", 1, 1, 0),
    ("send", "i", "s", "A", 3, -1, 0), ("send", "i", "s", "B", 1, -1, 1), ("send", "t", "z", 1, -1, 1),
    ("send", "i", "s", "A", 1, -1, 1), ("send", "t", "z", 1, 1, 2), ("send", "i", "s", "A", 3, -1, 1),
    ("send", "t", "c", 7, 1), ("send", "t", "z", 2, -1, 2), ("send", "t", "z", 2, 1, 0),
    ("send", "i", "s", "A", 2, 1, 0), ("send", "i", "s", "B", 2, 1, 0), ("send", "t", "c", 0, 0),
    ("send", "i", "s", "A", 3, 1, 1), ("send", "t", "z", 2, -1, 3), ("send", "t", "z", 2, 1, 1),
    ("send", "t", "c", 0, 1), ("send", "t", "c", 2, 1), ("send", "i", "s", "B", 2, -1, 0),
    ("send", "i", "s", "A", 2, -1, 0), ("send", "t", "c", 6, 0), ("send", "i", "sq", "A", 3, 1, 0),
    ("send", "t", "c", 1, 0), ("send", "i", "s", "B", 1, 1, 0), ("send", "t", "z", 2, -1, 0),
    ("send", "i", "s", "B", 2, -1, 1), ("send", "i", "sq", "B", 3, 1, 0), ("send", "t", "z", 2, 1, 3),
    ("send", "i", "sq", "B", 0, -1, 0), ("send", "i", "s", "A", 2, -1, 1), ("send", "t", "z", 2, -1, 1),
    ("send", "i", "sq", "A", 3, -1, 0), ("send", "i", "s", "B", 2, 1, 1), ("send", "i", "sq", "A", 0, 1, 0),
    ("send", "t", "z", 2, 1, 2), ("coef", 0, 384, 0, 384), ("send", "i", "sq", "B", 3, -1, 0),
    ("send", "i", "sq", "A", 1, -1, 0), ("send", "i", "s", "A", 2, 1, 1), ("send", "i", "sq", "B", 1, -1, 0),
    ("send", "i", "sq", "A", 1, 1, 0), ("send", "t", "c", 2, 0), ("send", "t", "z", 3, -1, 2),
    ("send", "t", "z", 3, 1, 0), ("send", "i", "sq", "B", 2, 1, 0), ("send", "i", "sq", "A", 2, 1, 0),
    ("send", "t", "z", 3, -1, 3), ("send", "t", "z", 3, 1, 1), ("send", "t", "c", 5, 0), ("send", "t", "c", 6, 1),
    ("send", "t", "c", 3, 1), ("send", "i", "sq", "B", 1, 1, 0), ("send", "i", "sq", "B", 2, -1, 0),
    ("send", "i", "sq", "A", 2, -1, 0), ("coef", 0, 384, 384, 256), ("send", "t", "c", 3, 0),
    ("send", "t", "c", 5, 1), ("coef", 384, 256, 0, 640), ("own",), ("coef", 640, 256, 0, 896),
    ("send", "t", "c", 4, 1), ("send", "t", "c", 4, 0), ("coef", 0, 640, 640, 256), ("coef", 0, 896, 896, 128),
    ("coef", 896, 128, 0, 1024), ("txt", 896, 128), ("give", "t", "c", 4, 0), ("give", "t", "c", 4, 1),
    ("img", 896, 128), ("give", "i", "sq", "A", 2, -1, 0), ("give", "i", "sq", "B", 2, -1, 0),
    ("give", "i", "sq", "A", 2, 1, 0), ("give", "i", "sq", "B", 2, 1, 0), ("give", "i", "sq", "A", 1, 1, 0),
    ("img", 768, 128), ("give", "i", "sq", "B", 1, 1, 0), ("give", "i", "sq", "B", 1, -1, 0),
    ("give", "t", "z", 3, 1, 0), ("give", "i", "sq", "A", 1, -1, 0), ("give", "t", "z", 3, -1, 2), ("txt", 640, 256),
    ("give", "t", "c", 5, 1), ("give", "t", "z", 3, -1, 3), ("give", "t", "z", 3, 1, 1), ("give", "t", "c", 3, 0),
    ("give", "i", "sq", "B", 3, 1, 0), ("give", "i", "sq", "A", 3, 1, 0), ("give", "i", "sq", "A", 3, -1, 0),
    ("give", "i", "sq", "B", 3, -1, 0), ("img", 512, 256), ("give", "t", "z", 2, 1, 2), ("give", "t", "z", 2, -1, 0),
    ("give", "i", "s", "A", 2, 1, 1), ("give", "t", "z", 2, -1, 1), ("give", "t", "c", 3, 1),
    ("give", "i", "s", "B", 2, 1, 1), ("give", "t", "z", 2, 1, 3), ("give", "t", "c", 5, 0),
    ("give", "i", "s", "A", 2, -1, 1), ("give", "i", "s", "B", 2, -1, 1), ("txt", 384, 256),
    ("give", "i", "s", "A", 2, -1, 0), ("give", "i", "s", "A", 2, 1, 0), ("give", "i", "s", "B", 2, -1, 0),
    ("give", "i", "s", "B", 2, 1, 0), ("give", "i", "sq", "B", 0, 1, 0), ("give", "i", "sq", "A", 0, 1, 0),
    ("give", "t", "c", 2, 0), ("give", "i", "s", "A", 1, -1, 1), ("give", "i", "sq", "B", 0, -1, 0),
    ("give", "t", "z", 2, 1, 0), ("give", "i", "sq", "A", 0, -1, 0), ("give", "t", "z", 2, -1, 2), ("img", 256, 256),
    ("give", "t", "z", 2, -1, 3), ("give", "t", "z", 2, 1, 1), ("give", "i", "s", "A", 1, 1, 0),
    ("give", "i", "s", "B", 3, 1, 1), ("give", "i", "s", "B", 1, -1, 1), ("give", "t", "c", 6, 1),
    ("give", "i", "s", "B", 3, 1, 0), ("txt", 128, 256), ("give", "i", "s", "A", 3, -1, 1),
    ("give", "i", "s", "A", 1, 1, 1), ("give", "i", "s", "B", 3, -1, 1), ("give", "t", "c", 6, 0),
    ("give", "i", "s", "B", 1, 1, 0), ("give", "t", "z", 1, -1, 0), ("give", "t", "z", 1, 1, 2),
    ("give", "i", "s", "A", 1, -1, 0), ("give", "i", "s", "A", 3, 1, 0), ("give", "i", "s", "A", 3, 1, 1),
    ("give", "i", "s", "A", 3, -1, 0), ("give", "i", "s", "B", 3, -1, 0), ("give", "t", "c", 2, 1),
    ("give", "i", "s", "B", 1, 1, 1), ("give", "i", "s", "B", 1, -1, 0), ("give", "t", "z", 1, 1, 3),
    ("give", "t", "z", 1, -1, 1), ("img", 0, 256), ("give", "t", "z", 1, -1, 2), ("give", "t", "z", 1, 1, 0),
    ("give", "i", "fq", "B", 0, -1, 0), ("give", "t", "c", 1, 0), ("give", "i", "fq", "A", 0, -1, 0),
    ("give", "i", "fq", "A", 0, 1, 0), ("give", "i", "fq", "B", 0, 1, 0), ("give", "i", "s", "A", 0, 1, 1),
    ("give", "i", "s", "B", 0, 1, 1), ("give", "t", "c", 7, 0), ("give", "t", "c", 1, 1), ("give", "t", "c", 7, 1),
    ("give", "t", "z", 1, -1, 3), ("give", "t", "z", 1, 1, 1), ("give", "i", "s", "B", 0, 1, 0), ("txt", 0, 128),
    ("give", "i", "s", "A", 0, -1, 0), ("give", "i", "s", "A", 0, 1, 0), ("give", "i", "f", "A", 0, -1, 1),
    ("give", "i", "s", "B", 0, -1, 1), ("give", "t", "z", 0, -1, 0), ("give", "t", "z", 0, 1, 2),
    ("give", "t", "c", 0, 0), ("give", "i", "s", "A", 0, -1, 1), ("give", "t", "z", 0, -1, 1),
    ("give", "t", "z", 0, 1, 3), ("give", "t", "c", 0, 1), ("give", "i", "f", "B", 0, -1, 1),
    ("give", "i", "f", "A", 0, 1, 1), ("give", "i", "f", "B", 0, 1, 1), ("give", "i", "s", "B", 0, -1, 0),
    ("give", "t", "z", 0, -1, 2), ("give", "t", "z", 0, 1, 0), ("give", "i", "f", "B", 0, -1, 0),
    ("give", "i", "f", "B", 0, 1, 0), ("give", "i", "f", "A", 0, -1, 0), ("give", "i", "f", "A", 0, 1, 0),
    ("give", "t", "z", 0, -1, 3), ("give", "t", "z", 0, 1, 1),
)

class Edge:
    def __init__(self, src, dst, row, count, axis, sign):
        self.src, self.dst, self.row, self.count = src, dst, row, count
        self.axis, self.sign = axis, sign


def img_edges():
    edges = {}
    for half, first, second in (("A", "x", "y"), ("B", "y", "x")):
        base = 0 if half == "A" else HALF

        def at(df, ds, first=first):
            return (df % 4, ds % 4) if first == "x" else (ds % 4, df % 4)

        for sg in (1, -1):
            rows = (base, base + QUARTER) if sg == 1 else (base + QUARTER, base)
            for i in (0, 1):
                edges["f", half, 0, sg, i] = Edge(at(0, 0), at(-sg, 0), rows[i], QUARTER, first, sg)
            edges["fq", half, 0, sg, 0] = Edge(at(-sg, 0), at(2, 0), rows[0], QUARTER, first, sg)
            for df in range(4):
                for i in (0, 1):
                    edges["s", half, df, sg, i] = Edge(at(df, 0), at(df, -sg), rows[i], QUARTER, second, sg)
                edges["sq", half, df, sg, 0] = Edge(at(df, -sg), at(df, 2), rows[0], QUARTER, second, sg)
    return edges


def txt_edges():
    edges = {}
    for sg in (1, -1):
        for k in range(4):
            for c in CHUNKS[sg][: 4 if k < 3 else 2]:
                edges["z", k, sg, c] = Edge(
                    ((-sg * k) % NZ, 0), ((-sg * (k + 1)) % NZ, 0), c * QUARTER, QUARTER, "z", sg
                )
    for dz in range(NZ):
        for h in (0, 1):
            edges["c", dz, h] = Edge((dz, 0), (dz, 1), h * HALF, HALF, "c", 1)
    return edges


class Side:
    def __init__(self, units, edges, rows, part, out, back, sems, place):
        self.unit = 16 * ROWS // len(units)
        self.at = {unit: i * self.unit for i, unit in enumerate(units)}
        self.done = set()
        self.edges = edges
        self.number = {key: i for i, key in enumerate(edges)}
        self.rows, self.part, self.out, self.back = rows, part, out, back
        self.g_send, self.g_recv, self.r_send, self.r_recv = sems
        self.place = place
        self.sent, self.returned = set(), set()
        self.seen, self.taken = set(), set()

    def span(self, slot, row, count):
        return pl.ds(self.at[slot, row // self.unit] + row % self.unit, count)

    def gather_copy(self, key):
        e, i = self.edges[key], self.number[key]
        return pltpu.make_async_remote_copy(
            src_ref=self.rows.at[self.span(e.src, e.row, e.count)],
            dst_ref=self.rows.at[self.span(e.dst, e.row, e.count)],
            send_sem=self.g_send.at[i],
            recv_sem=self.g_recv.at[i],
            device_id=self.place(e.axis, e.sign),
            device_id_type=MESH,
        )

    def scatter_copy(self, key):
        e, i = self.edges[key], self.number[key]
        where = self.span(e.dst, e.row, e.count)
        return pltpu.make_async_remote_copy(
            src_ref=self.out.at[where],
            dst_ref=self.back.at[where],
            send_sem=self.r_send.at[i],
            recv_sem=self.r_recv.at[i],
            device_id=self.place(e.axis, -e.sign),
            device_id_type=MESH,
        )

    def send(self, *keys):
        for key in keys:
            e = self.edges[key]
            self.arrive(e.src, e.row, e.count)
            self.gather_copy(key).start()
            self.sent.add(key)

    def arrive_until(self, end):
        for (slot, which), start in self.at.items():
            if start < end:
                self.arrive(slot, which * self.unit, self.unit)

    def arrive(self, slot, row=0, count=ROWS):
        for key, e in self.edges.items():
            if e.dst == slot and e.row < row + count and row < e.row + e.count and key not in self.seen:
                assert key in self.sent, key
                self.gather_copy(key).wait_recv()
                self.seen.add(key)

    def total(self, slot, row, count):
        assert self.span(slot, row, count).start in self.done
        value = self.part[self.span(slot, row, count), :]
        for key, e in self.edges.items():
            if e.src == slot and e.row <= row and row + count <= e.row + e.count:
                if key not in self.taken:
                    assert key in self.returned, key
                    self.scatter_copy(key).wait_recv()
                    self.taken.add(key)
                value = value + self.back[self.span(e.dst, row, count), :].astype(jnp.float32)
        return value

    def passed(self, slot, row):
        return any(e.src == slot and e.row <= row < e.row + e.count for e in self.edges.values())

    def store(self, value, start):
        for (slot, which), first in self.at.items():
            if not start <= first < start + value.shape[0]:
                continue
            for row in range(0, self.unit, QUARTER):
                at = first + row
                rows = value[at - start:at - start + QUARTER, :]
                if self.passed(slot, which * self.unit + row):
                    self.part[at:at + QUARTER, :] = rows
                else:
                    self.out[at:at + QUARTER, :] = rows.astype(jnp.bfloat16)
                self.done.add(at)

    def give(self, *keys):
        for key in keys:
            e = self.edges[key]
            for row in range(e.row, e.row + e.count, QUARTER):
                where = self.span(e.dst, row, QUARTER)
                assert where.start in self.done
                if self.passed(e.dst, row):
                    self.out[where, :] = self.total(e.dst, row, QUARTER).astype(jnp.bfloat16)
            self.scatter_copy(key).start()
            self.returned.add(key)

    def take(self, last):
        own = {
            key: e for key, e in self.edges.items() if e.src == (0, 0) and (key[0] in ("f", "z")) == last
        }
        for key in own:
            assert key in self.returned
            self.scatter_copy(key).wait_recv()
            self.taken.add(key)
        for row in range(0, ROWS, QUARTER):
            value = self.part[self.span((0, 0), row, QUARTER), :]
            for e in own.values():
                if e.row <= row and row + QUARTER <= e.row + e.count:
                    value = value + self.back[self.span(e.dst, row, QUARTER), :].astype(jnp.float32)
            self.part[self.span((0, 0), row, QUARTER), :] = value

    def settle(self):
        for key in self.edges:
            self.gather_copy(key).wait_send()
            if self.edges[key].src != (0, 0):
                self.scatter_copy(key).wait_send()

    def finish(self):
        assert len(self.sent) == len(self.returned) == len(self.seen) == len(self.taken) == len(self.edges)
        for key in self.edges:
            if self.edges[key].src == (0, 0):
                self.scatter_copy(key).wait_send()


def unit_of(emb):
    wide = emb.astype(jnp.float32)
    inverse = lax.rsqrt(jnp.sum(wide * wide, axis=1, keepdims=True) + EPS)
    return wide * inverse, inverse


def back_norm(unit, inverse, grad):
    return inverse * (grad - unit * jnp.sum(unit * grad, axis=1, keepdims=True))


def kernel(
    img_hbm, txt_hbm, temp_hbm, bias_hbm, img_out, txt_out,
    img_ref, txt_ref, temp_ref, bias_ref, in_sems, img_unit, txt_unit, img_inv, txt_inv,
    p_rows, q_rows, coef, p_part, q_part, p_send, q_send, p_back, q_back,
    pg_send, pg_recv, pr_send, pr_recv, qg_send, qg_recv, qr_send, qr_recv,
):
    loads = [
        pltpu.make_async_copy(here, there, in_sems.at[i])
        for i, (here, there) in enumerate(
            ((img_hbm, img_ref), (txt_hbm, txt_ref), (temp_hbm, temp_ref), (bias_hbm, bias_ref))
        )
    ]
    for load in loads:
        load.start()
    dp, mp = lax.axis_index("dp"), lax.axis_index("mp")
    core, z, x = dp % 2, (dp // 2) % NZ, (dp // (2 * NZ)) * 2 + mp // NY
    y = mp % NY

    @functools.cache
    def place(axis, sign):
        nx, ny, nz, nc = x, y, z, core
        if axis == "x":
            nx = (x + sign + NX) % NX
        elif axis == "y":
            ny = (y + sign + NY) % NY
        elif axis == "z":
            nz = (z + sign + NZ) % NZ
        else:
            nc = 1 - core
        return ((nx // 2) * (2 * NZ) + nz * 2 + nc, (nx % 2) * NY + ny)

    barrier = pltpu.get_barrier_semaphore()
    neighbours = [place(a, s) for a in "xyz" for s in (1, -1)] + [place("c", 1)]
    for device in neighbours:
        pl.semaphore_signal(barrier, inc=1, device_id=device, device_id_type=MESH)

    img = Side(IMG_UNITS, img_edges(), p_rows, p_part, p_send, p_back,
               (pg_send, pg_recv, pr_send, pr_recv), place)
    txt = Side(TXT_UNITS, txt_edges(), q_rows, q_part, q_send, q_back,
               (qg_send, qg_recv, qr_send, qr_recv), place)

    loads[0].wait()
    unit, inverse = unit_of(img_ref[...])
    p_rows[0:ROWS, :] = unit.astype(jnp.bfloat16)
    img_unit[...] = unit
    img_inv[...] = jnp.broadcast_to(inverse, img_inv.shape)
    pl.semaphore_wait(barrier, len(neighbours))
    for sg in (1, -1):
        for half in "AB":
            img.send(("f", half, 0, sg, 0))
    for load in loads[1:]:
        load.wait()
    half_tau = 0.5 * jnp.exp(temp_ref[...].reshape(1, 1))
    half_bias = 0.5 * bias_ref[...].reshape(1, 1)

    unit, inverse = unit_of(txt_ref[...])
    q_rows[0:ROWS, :] = unit.astype(jnp.bfloat16)
    txt_unit[...] = unit
    txt_inv[...] = jnp.broadcast_to(inverse, txt_inv.shape)

    def scores(t0, tn, i0, n):
        txt.arrive_until(t0 + tn)
        img.arrive_until(i0 + n)
        dots = lax.dot_general(q_rows[t0:t0 + tn, :], p_rows[i0:i0 + n, :], NT,
                               preferred_element_type=jnp.float32)
        wave = jnp.tanh(half_tau * dots + half_bias)
        coef[t0:t0 + tn, i0:i0 + n] = (half_tau * wave + half_tau).astype(jnp.bfloat16)

    def own_scores():
        dots = lax.dot_general(q_rows[0:ROWS, :], p_rows[0:128, :], NT,
                               preferred_element_type=jnp.float32)
        wave = jnp.tanh(half_tau * dots + half_bias)
        same = lax.broadcasted_iota(jnp.int32, dots.shape, 0) == lax.broadcasted_iota(jnp.int32, dots.shape, 1)
        coef[0:ROWS, 0:128] = (half_tau * wave + jnp.where(same, -half_tau, half_tau)).astype(jnp.bfloat16)

    def img_grads(i0, n):
        img.store(lax.dot_general(coef[:, i0:i0 + n], q_rows[...], TN, preferred_element_type=jnp.float32), i0)

    def txt_grads(t0, n):
        txt.store(lax.dot_general(coef[t0:t0 + n, :], p_rows[...], NN, preferred_element_type=jnp.float32), t0)

    sides = {"i": img, "t": txt}
    for step in PLAN:
        if step[0] == "send" and (step[1] != "i" or step[2:] not in img.sent):
            sides[step[1]].send(step[2:])
        elif step[0] == "send":
            pass
        elif step[0] == "give":
            sides[step[1]].give(step[2:])
        elif step[0] == "coef":
            scores(*step[1:])
        elif step[0] == "own":
            assert ("coef", 0, 384, 0, 384) in PLAN[: PLAN.index(step)]
            own_scores()
        elif step[0] == "img":
            img_grads(*step[1:])
        else:
            txt_grads(*step[1:])

    for side in (img, txt):
        side.settle()
        side.take(last=False)
    for side, unit, inverse, out in ((img, img_unit, img_inv, img_out), (txt, txt_unit, txt_inv, txt_out)):
        side.take(last=True)
        out[...] = back_norm(unit[...], inverse[:, 0:1], side.part[0:ROWS, :])
    img.finish()
    txt.finish()


def store_kernel(img_ref, txt_ref, img_out, txt_out, sems):
    stores = [
        pltpu.make_async_copy(here, there, sems.at[i])
        for i, (here, there) in enumerate(((img_ref, img_out), (txt_ref, txt_out)))
    ]
    for store in stores:
        store.start()
    for store in stores:
        store.wait()


def on_device(image_emb, text_emb, log_temp, bias):
    rows, width = image_emb.shape
    group = 16 * rows
    n_img, n_txt = len(img_edges()), len(txt_edges())
    vmem = pl.BlockSpec(memory_space=pltpu.VMEM)
    hbm = pl.BlockSpec(memory_space=pltpu.HBM)
    grads = pl.pallas_call(
        kernel,
        out_shape=[pltpu.VMEM((rows, width), jnp.float32)] * 2,
        in_specs=[pl.BlockSpec(memory_space=pl.ANY)] * 4,
        out_specs=[vmem, vmem],
        scratch_shapes=(
            [pltpu.VMEM((rows, width), jnp.bfloat16)] * 2
            + [pltpu.VMEM((1,), jnp.float32)] * 2
            + [pltpu.SemaphoreType.DMA((4,))]
            + [pltpu.VMEM((rows, width), jnp.float32)] * 2
            + [pltpu.VMEM((rows, 128), jnp.float32)] * 2
            + [pltpu.VMEM((group, width), jnp.bfloat16)] * 2
            + [pltpu.VMEM((group, group), jnp.bfloat16)]
            + [pltpu.VMEM((group, width), jnp.float32)] * 2
            + [pltpu.VMEM((group, width), jnp.bfloat16)] * 4
            + [pltpu.SemaphoreType.DMA((n_img,))] * 4
            + [pltpu.SemaphoreType.DMA((n_txt,))] * 4
        ),
        compiler_params=pltpu.CompilerParams(
            collective_id=0, has_side_effects=True, vmem_limit_bytes=56 * 2**20
        ),
    )(image_emb, text_emb, log_temp, bias)
    anywhere = pl.BlockSpec(memory_space=pl.ANY)
    return pl.pallas_call(
        store_kernel,
        out_shape=[jax.ShapeDtypeStruct((rows, width), jnp.float32)] * 2,
        in_specs=[vmem] * 2,
        out_specs=[anywhere] * 2,
        scratch_shapes=[pltpu.SemaphoreType.DMA((2,))],
    )(*(pltpu.with_memory_space_constraint(grad, pltpu.VMEM) for grad in grads))


def solution(mesh):
    placed = (P(("dp", "mp"), None), P(("dp", "mp"), None), P(), P())
    return jax.shard_map(
        on_device,
        mesh=mesh,
        in_specs=placed,
        out_specs=(P(("dp", "mp"), None), P(("dp", "mp"), None)),
        check_vma=False,
    )
```

```python
import functools

import jax
import jax.numpy as jnp
from jax import lax
from jax.experimental import pallas as pl
from jax.experimental.pallas import tpu as pltpu
from jax.sharding import PartitionSpec as P

EPS = 1e-06
MESH = pl.DeviceIdType.MESH
NX, NY, NZ = 4, 4, 8
ROWS = 64
HALF = ROWS // 2
QUARTER = ROWS // 4
NT = (((1,), (1,)), ((), ()))
TN = (((0,), (0,)), ((), ()))
NN = (((1,), (0,)), ((), ()))
CHUNKS = {1: (0, 1, 2, 3), -1: (2, 3, 0, 1)}

IMG_UNITS = (
    [((0, 0), 0), ((0, 0), 1)]
    + [((d, 0), 0) for d in (1, 3)] + [((0, d), 1) for d in (1, 3)]
    + [((0, d), 0) for d in (1, 3)] + [((d, 0), 1) for d in (1, 3)]
    + [((2, 0), 0), ((0, 2), 1)]
    + [((3, d), 0) for d in (1, 3)] + [((d, 3), 1) for d in (1, 3)]
    + [((1, d), 0) for d in (1, 3)] + [((d, 1), 1) for d in (1, 3)]
    + [((2, d), 0) for d in (1, 3)] + [((d, 2), 1) for d in (1, 3)]
    + [((0, 2), 0), ((2, 0), 1)]
    + [((3, 2), 0), ((2, 3), 1), ((1, 2), 0), ((2, 1), 1), ((2, 2), 0), ((2, 2), 1)]
)
TXT_UNITS = [((dz, s), 0) for dz in (0, 1, 7, 2, 6, 3, 5, 4) for s in (0, 1)]


PLAN = (
    ("send", "t", "z", 0, -1, 2), ("send", "t", "z", 0, 1, 0), ("send", "t", "z", 0, -1, 3),
    ("send", "i", "f", "A", 0, 1, 0), ("send", "i", "f", "B", 0, -1, 0), ("send", "t", "z", 0, 1, 1),
    ("send", "i", "f", "B", 0, 1, 0), ("send", "i", "f", "A", 0, -1, 0), ("send", "t", "z", 0, -1, 0),
    ("send", "i", "f", "A", 0, 1, 1), ("send", "t", "z", 0, 1, 3), ("send", "i", "s", "A", 0, -1, 0),
    ("send", "i", "s", "B", 0, -1, 1), ("send", "t", "z", 0, 1, 2), ("send", "i", "f", "B", 0, -1, 1),
    ("send", "i", "s", "B", 0, 1, 0), ("send", "i", "s", "A", 0, 1, 1), ("send", "i", "f", "B", 0, 1, 1),
    ("send", "i", "s", "A", 0, 1, 0), ("send", "i", "s", "B", 0, 1, 1), ("send", "i", "f", "A", 0, -1, 1),
    ("send", "i", "s", "B", 0, -1, 0), ("send", "i", "s", "A", 0, -1, 1), ("send", "t", "z", 0, -1, 1),
    ("send", "t", "z", 1, -1, 2), ("send", "t", "z", 1, 1, 0), ("send", "i", "fq", "A", 0, 1, 0),
    ("send", "i", "fq", "B", 0, -1, 0), ("send", "i", "s", "A", 1, -1, 0), ("send", "i", "fq", "A", 0, -1, 0),
    ("send", "i", "fq", "B", 0, 1, 0), ("send", "i", "s", "B", 1, 1, 1), ("send", "i", "s", "B", 3, -1, 1),
    ("send", "t", "z", 1, -1, 3), ("send", "t", "z", 1, 1, 1), ("send", "i", "s", "B", 3, 1, 0),
    ("send", "i", "sq", "A", 0, -1, 0), ("send", "i", "s", "B", 1, -1, 0), ("send", "i", "s", "A", 3, 1, 0),
    ("send", "t", "z", 1, -1, 0), ("send", "i", "sq", "B", 0, 1, 0), ("send", "t", "c", 1, 1),
    ("send", "t", "z", 1, 1, 3), ("send", "t", "c", 7, 0), ("send", "i", "s", "B", 3, -1, 0),
    ("send", "i", "s", "B", 3, 1, 1), ("send", "i", "s", "A", 1, 1, 1), ("send", "i", "s", "A", 1, 1, 0),
    ("send", "i", "s", "A", 3, -1, 0), ("send", "i", "s", "B", 1, -1, 1), ("send", "t", "z", 1, -1, 1),
    ("send", "i", "s", "A", 1, -1, 1), ("send", "t", "z", 1, 1, 2), ("send", "i", "s", "A", 3, -1, 1),
    ("send", "t", "c", 7, 1), ("send", "t", "z", 2, -1, 2), ("send", "t", "z", 2, 1, 0),
    ("send", "i", "s", "A", 2, 1, 0), ("send", "i", "s", "B", 2, 1, 0), ("send", "t", "c", 0, 0),
    ("send", "i", "s", "A", 3, 1, 1), ("send", "t", "z", 2, -1, 3), ("send", "t", "z", 2, 1, 1),
    ("send", "t", "c", 0, 1), ("send", "t", "c", 2, 1), ("send", "i", "s", "B", 2, -1, 0),
    ("send", "i", "s", "A", 2, -1, 0), ("send", "t", "c", 6, 0), ("send", "i", "sq", "A", 3, 1, 0),
    ("send", "t", "c", 1, 0), ("send", "i", "s", "B", 1, 1, 0), ("send", "t", "z", 2, -1, 0),
    ("send", "i", "s", "B", 2, -1, 1), ("send", "i", "sq", "B", 3, 1, 0), ("send", "t", "z", 2, 1, 3),
    ("send", "i", "sq", "B", 0, -1, 0), ("send", "i", "s", "A", 2, -1, 1), ("send", "t", "z", 2, -1, 1),
    ("send", "i", "sq", "A", 3, -1, 0), ("send", "i", "s", "B", 2, 1, 1), ("send", "i", "sq", "A", 0, 1, 0),
    ("send", "t", "z", 2, 1, 2), ("coef", 0, 384, 0, 384), ("send", "i", "sq", "B", 3, -1, 0),
    ("send", "i", "sq", "A", 1, -1, 0), ("send", "i", "s", "A", 2, 1, 1), ("send", "i", "sq", "B", 1, -1, 0),
    ("send", "i", "sq", "A", 1, 1, 0), ("send", "t", "c", 2, 0), ("send", "t", "z", 3, -1, 2),
    ("send", "t", "z", 3, 1, 0), ("send", "i", "sq", "B", 2, 1, 0), ("send", "i", "sq", "A", 2, 1, 0),
    ("send", "t", "z", 3, -1, 3), ("send", "t", "z", 3, 1, 1), ("send", "t", "c", 5, 0), ("send", "t", "c", 6, 1),
    ("send", "t", "c", 3, 1), ("send", "i", "sq", "B", 1, 1, 0), ("send", "i", "sq", "B", 2, -1, 0),
    ("send", "i", "sq", "A", 2, -1, 0), ("coef", 0, 384, 384, 256), ("send", "t", "c", 3, 0),
    ("send", "t", "c", 5, 1), ("coef", 384, 256, 0, 640), ("own",), ("coef", 640, 256, 0, 896),
    ("send", "t", "c", 4, 1), ("send", "t", "c", 4, 0), ("coef", 0, 640, 640, 256), ("coef", 0, 896, 896, 128),
    ("coef", 896, 128, 0, 1024), ("txt", 896, 128), ("give", "t", "c", 4, 0), ("give", "t", "c", 4, 1),
    ("img", 896, 128), ("give", "i", "sq", "A", 2, -1, 0), ("give", "i", "sq", "B", 2, -1, 0),
    ("give", "i", "sq", "A", 2, 1, 0), ("give", "i", "sq", "B", 2, 1, 0), ("give", "i", "sq", "A", 1, 1, 0),
    ("img", 768, 128), ("give", "i", "sq", "B", 1, 1, 0), ("give", "i", "sq", "B", 1, -1, 0),
    ("give", "t", "z", 3, 1, 0), ("give", "i", "sq", "A", 1, -1, 0), ("give", "t", "z", 3, -1, 2), ("txt", 640, 256),
    ("give", "t", "c", 5, 1), ("give", "t", "z", 3, -1, 3), ("give", "t", "z", 3, 1, 1), ("give", "t", "c", 3, 0),
    ("give", "i", "sq", "B", 3, 1, 0), ("give", "i", "sq", "A", 3, 1, 0), ("give", "i", "sq", "A", 3, -1, 0),
    ("give", "i", "sq", "B", 3, -1, 0), ("img", 512, 256), ("give", "t", "z", 2, 1, 2), ("give", "t", "z", 2, -1, 0),
    ("give", "i", "s", "A", 2, 1, 1), ("give", "t", "z", 2, -1, 1), ("give", "t", "c", 3, 1),
    ("give", "i", "s", "B", 2, 1, 1), ("give", "t", "z", 2, 1, 3), ("give", "t", "c", 5, 0),
    ("give", "i", "s", "A", 2, -1, 1), ("give", "i", "s", "B", 2, -1, 1), ("txt", 384, 256),
    ("give", "i", "s", "A", 2, -1, 0), ("give", "i", "s", "A", 2, 1, 0), ("give", "i", "s", "B", 2, -1, 0),
    ("give", "i", "s", "B", 2, 1, 0), ("give", "i", "sq", "B", 0, 1, 0), ("give", "i", "sq", "A", 0, 1, 0),
    ("give", "t", "c", 2, 0), ("give", "i", "s", "A", 1, -1, 1), ("give", "i", "sq", "B", 0, -1, 0),
    ("give", "t", "z", 2, 1, 0), ("give", "i", "sq", "A", 0, -1, 0), ("give", "t", "z", 2, -1, 2), ("img", 256, 256),
    ("give", "t", "z", 2, -1, 3), ("give", "t", "z", 2, 1, 1), ("give", "i", "s", "A", 1, 1, 0),
    ("give", "i", "s", "B", 3, 1, 1), ("give", "i", "s", "B", 1, -1, 1), ("give", "t", "c", 6, 1),
    ("give", "i", "s", "B", 3, 1, 0), ("txt", 128, 256), ("give", "i", "s", "A", 3, -1, 1),
    ("give", "i", "s", "A", 1, 1, 1), ("give", "i", "s", "B", 3, -1, 1), ("give", "t", "c", 6, 0),
    ("give", "i", "s", "B", 1, 1, 0), ("give", "t", "z", 1, -1, 0), ("give", "t", "z", 1, 1, 2),
    ("give", "i", "s", "A", 1, -1, 0), ("give", "i", "s", "A", 3, 1, 0), ("give", "i", "s", "A", 3, 1, 1),
    ("give", "i", "s", "A", 3, -1, 0), ("give", "i", "s", "B", 3, -1, 0), ("give", "t", "c", 2, 1),
    ("give", "i", "s", "B", 1, 1, 1), ("give", "i", "s", "B", 1, -1, 0), ("give", "t", "z", 1, 1, 3),
    ("give", "t", "z", 1, -1, 1), ("img", 0, 256), ("give", "t", "z", 1, -1, 2), ("give", "t", "z", 1, 1, 0),
    ("give", "i", "fq", "B", 0, -1, 0), ("give", "t", "c", 1, 0), ("give", "i", "fq", "A", 0, -1, 0),
    ("give", "i", "fq", "A", 0, 1, 0), ("give", "i", "fq", "B", 0, 1, 0), ("give", "i", "s", "A", 0, 1, 1),
    ("give", "i", "s", "B", 0, 1, 1), ("give", "t", "c", 7, 0), ("give", "t", "c", 1, 1), ("give", "t", "c", 7, 1),
    ("give", "t", "z", 1, -1, 3), ("give", "t", "z", 1, 1, 1), ("give", "i", "s", "B", 0, 1, 0), ("txt", 0, 128),
    ("give", "i", "s", "A", 0, -1, 0), ("give", "i", "s", "A", 0, 1, 0), ("give", "i", "f", "A", 0, -1, 1),
    ("give", "i", "s", "B", 0, -1, 1), ("give", "t", "z", 0, -1, 0), ("give", "t", "z", 0, 1, 2),
    ("give", "t", "c", 0, 0), ("give", "i", "s", "A", 0, -1, 1), ("give", "t", "z", 0, -1, 1),
    ("give", "t", "z", 0, 1, 3), ("give", "t", "c", 0, 1), ("give", "i", "f", "B", 0, -1, 1),
    ("give", "i", "f", "A", 0, 1, 1), ("give", "i", "f", "B", 0, 1, 1), ("give", "i", "s", "B", 0, -1, 0),
    ("give", "t", "z", 0, -1, 2), ("give", "t", "z", 0, 1, 0), ("give", "i", "f", "B", 0, -1, 0),
    ("give", "i", "f", "B", 0, 1, 0), ("give", "i", "f", "A", 0, -1, 0), ("give", "i", "f", "A", 0, 1, 0),
    ("give", "t", "z", 0, -1, 3), ("give", "t", "z", 0, 1, 1),
)

class Edge:
    def __init__(self, src, dst, row, count, axis, sign):
        self.src, self.dst, self.row, self.count = src, dst, row, count
        self.axis, self.sign = axis, sign


def img_edges():
    edges = {}
    for half, first, second in (("A", "x", "y"), ("B", "y", "x")):
        base = 0 if half == "A" else HALF

        def at(df, ds, first=first):
            return (df % 4, ds % 4) if first == "x" else (ds % 4, df % 4)

        for sg in (1, -1):
            rows = (base, base + QUARTER) if sg == 1 else (base + QUARTER, base)
            for i in (0, 1):
                edges["f", half, 0, sg, i] = Edge(at(0, 0), at(-sg, 0), rows[i], QUARTER, first, sg)
            edges["fq", half, 0, sg, 0] = Edge(at(-sg, 0), at(2, 0), rows[0], QUARTER, first, sg)
            for df in range(4):
                for i in (0, 1):
                    edges["s", half, df, sg, i] = Edge(at(df, 0), at(df, -sg), rows[i], QUARTER, second, sg)
                edges["sq", half, df, sg, 0] = Edge(at(df, -sg), at(df, 2), rows[0], QUARTER, second, sg)
    return edges


def txt_edges():
    edges = {}
    for sg in (1, -1):
        for k in range(4):
            for c in CHUNKS[sg][: 4 if k < 3 else 2]:
                edges["z", k, sg, c] = Edge(
                    ((-sg * k) % NZ, 0), ((-sg * (k + 1)) % NZ, 0), c * QUARTER, QUARTER, "z", sg
                )
    for dz in range(NZ):
        for h in (0, 1):
            edges["c", dz, h] = Edge((dz, 0), (dz, 1), h * HALF, HALF, "c", 1)
    return edges


class Side:
    def __init__(self, units, edges, rows, part, out, back, sems, place):
        self.unit = 16 * ROWS // len(units)
        self.at = {unit: i * self.unit for i, unit in enumerate(units)}
        self.done = set()
        self.edges = edges
        self.number = {key: i for i, key in enumerate(edges)}
        self.rows, self.part, self.out, self.back = rows, part, out, back
        self.g_send, self.g_recv, self.r_send, self.r_recv = sems
        self.place = place
        self.sent, self.returned = set(), set()
        self.seen, self.taken = set(), set()

    def span(self, slot, row, count):
        return pl.ds(self.at[slot, row // self.unit] + row % self.unit, count)

    def gather_copy(self, key):
        e, i = self.edges[key], self.number[key]
        return pltpu.make_async_remote_copy(
            src_ref=self.rows.at[self.span(e.src, e.row, e.count)],
            dst_ref=self.rows.at[self.span(e.dst, e.row, e.count)],
            send_sem=self.g_send.at[i],
            recv_sem=self.g_recv.at[i],
            device_id=self.place(e.axis, e.sign),
            device_id_type=MESH,
        )

    def scatter_copy(self, key):
        e, i = self.edges[key], self.number[key]
        where = self.span(e.dst, e.row, e.count)
        return pltpu.make_async_remote_copy(
            src_ref=self.out.at[where],
            dst_ref=self.back.at[where],
            send_sem=self.r_send.at[i],
            recv_sem=self.r_recv.at[i],
            device_id=self.place(e.axis, -e.sign),
            device_id_type=MESH,
        )

    def send(self, *keys):
        for key in keys:
            e = self.edges[key]
            self.arrive(e.src, e.row, e.count)
            self.gather_copy(key).start()
            self.sent.add(key)

    def arrive_until(self, end):
        for (slot, which), start in self.at.items():
            if start < end:
                self.arrive(slot, which * self.unit, self.unit)

    def arrive(self, slot, row=0, count=ROWS):
        for key, e in self.edges.items():
            if e.dst == slot and e.row < row + count and row < e.row + e.count and key not in self.seen:
                assert key in self.sent, key
                self.gather_copy(key).wait_recv()
                self.seen.add(key)

    def total(self, slot, row, count):
        assert self.span(slot, row, count).start in self.done
        value = self.part[self.span(slot, row, count), :]
        for key, e in self.edges.items():
            if e.src == slot and e.row <= row and row + count <= e.row + e.count:
                if key not in self.taken:
                    assert key in self.returned, key
                    self.scatter_copy(key).wait_recv()
                    self.taken.add(key)
                value = value + self.back[self.span(e.dst, row, count), :].astype(jnp.float32)
        return value

    def passed(self, slot, row):
        return any(e.src == slot and e.row <= row < e.row + e.count for e in self.edges.values())

    def store(self, value, start):
        for (slot, which), first in self.at.items():
            if not start <= first < start + value.shape[0]:
                continue
            for row in range(0, self.unit, QUARTER):
                at = first + row
                rows = value[at - start:at - start + QUARTER, :]
                if self.passed(slot, which * self.unit + row):
                    self.part[at:at + QUARTER, :] = rows
                else:
                    self.out[at:at + QUARTER, :] = rows.astype(jnp.bfloat16)
                self.done.add(at)

    def give(self, *keys):
        for key in keys:
            e = self.edges[key]
            for row in range(e.row, e.row + e.count, QUARTER):
                where = self.span(e.dst, row, QUARTER)
                assert where.start in self.done
                if self.passed(e.dst, row):
                    self.out[where, :] = self.total(e.dst, row, QUARTER).astype(jnp.bfloat16)
            self.scatter_copy(key).start()
            self.returned.add(key)

    def take(self, last):
        own = {
            key: e for key, e in self.edges.items() if e.src == (0, 0) and (key[0] in ("f", "z")) == last
        }
        for key in own:
            assert key in self.returned
            self.scatter_copy(key).wait_recv()
            self.taken.add(key)
        for row in range(0, ROWS, QUARTER):
            value = self.part[self.span((0, 0), row, QUARTER), :]
            for e in own.values():
                if e.row <= row and row + QUARTER <= e.row + e.count:
                    value = value + self.back[self.span(e.dst, row, QUARTER), :].astype(jnp.float32)
            self.part[self.span((0, 0), row, QUARTER), :] = value

    def settle(self):
        for key in self.edges:
            self.gather_copy(key).wait_send()
            if self.edges[key].src != (0, 0):
                self.scatter_copy(key).wait_send()

    def finish(self):
        assert len(self.sent) == len(self.returned) == len(self.seen) == len(self.taken) == len(self.edges)
        for key in self.edges:
            if self.edges[key].src == (0, 0):
                self.scatter_copy(key).wait_send()


def unit_of(emb):
    wide = emb.astype(jnp.float32)
    inverse = lax.rsqrt(jnp.sum(wide * wide, axis=1, keepdims=True) + EPS)
    return wide * inverse, inverse


def back_norm(unit, inverse, grad):
    return inverse * (grad - unit * jnp.sum(unit * grad, axis=1, keepdims=True))


def kernel(
    img_hbm, txt_hbm, temp_hbm, bias_hbm, img_out, txt_out,
    img_ref, txt_ref, temp_ref, bias_ref, in_sems, img_unit, txt_unit, img_inv, txt_inv,
    p_rows, q_rows, coef, p_part, q_part, p_send, q_send, p_back, q_back,
    pg_send, pg_recv, pr_send, pr_recv, qg_send, qg_recv, qr_send, qr_recv,
):
    dp, mp = lax.axis_index("dp"), lax.axis_index("mp")
    core, z, x = dp % 2, (dp // 2) % NZ, (dp // (2 * NZ)) * 2 + mp // NY
    y = mp % NY

    @functools.cache
    def place(axis, sign):
        nx, ny, nz, nc = x, y, z, core
        if axis == "x":
            nx = (x + sign + NX) % NX
        elif axis == "y":
            ny = (y + sign + NY) % NY
        elif axis == "z":
            nz = (z + sign + NZ) % NZ
        else:
            nc = 1 - core
        return ((nx // 2) * (2 * NZ) + nz * 2 + nc, (nx % 2) * NY + ny)

    barrier = pltpu.get_barrier_semaphore()
    neighbours = [place(a, s) for a in "xyz" for s in (1, -1)] + [place("c", 1)]
    for device in neighbours:
        pl.semaphore_signal(barrier, inc=1, device_id=device, device_id_type=MESH)

    loads = [
        pltpu.make_async_copy(here, there, in_sems.at[i])
        for i, (here, there) in enumerate(
            ((img_hbm, img_ref), (txt_hbm, txt_ref), (temp_hbm, temp_ref), (bias_hbm, bias_ref))
        )
    ]
    for load in loads:
        load.start()
    img = Side(IMG_UNITS, img_edges(), p_rows, p_part, p_send, p_back,
               (pg_send, pg_recv, pr_send, pr_recv), place)
    txt = Side(TXT_UNITS, txt_edges(), q_rows, q_part, q_send, q_back,
               (qg_send, qg_recv, qr_send, qr_recv), place)

    loads[0].wait()
    unit, inverse = unit_of(img_ref[...])
    p_rows[0:ROWS, :] = unit.astype(jnp.bfloat16)
    img_unit[...] = unit
    img_inv[...] = jnp.broadcast_to(inverse, img_inv.shape)
    pl.semaphore_wait(barrier, len(neighbours))
    for sg in (1, -1):
        for half in "AB":
            img.send(("f", half, 0, sg, 0))
    for load in loads[1:]:
        load.wait()
    half_tau = 0.5 * jnp.exp(temp_ref[...].reshape(1, 1))
    half_bias = 0.5 * bias_ref[...].reshape(1, 1)

    unit, inverse = unit_of(txt_ref[...])
    q_rows[0:ROWS, :] = unit.astype(jnp.bfloat16)
    txt_unit[...] = unit
    txt_inv[...] = jnp.broadcast_to(inverse, txt_inv.shape)

    def scores(t0, tn, i0, n):
        txt.arrive_until(t0 + tn)
        img.arrive_until(i0 + n)
        dots = lax.dot_general(q_rows[t0:t0 + tn, :], p_rows[i0:i0 + n, :], NT,
                               preferred_element_type=jnp.float32)
        wave = jnp.tanh(half_tau * dots + half_bias)
        coef[t0:t0 + tn, i0:i0 + n] = (half_tau * wave + half_tau).astype(jnp.bfloat16)

    def own_scores():
        dots = lax.dot_general(q_rows[0:ROWS, :], p_rows[0:128, :], NT,
                               preferred_element_type=jnp.float32)
        wave = jnp.tanh(half_tau * dots + half_bias)
        same = lax.broadcasted_iota(jnp.int32, dots.shape, 0) == lax.broadcasted_iota(jnp.int32, dots.shape, 1)
        coef[0:ROWS, 0:128] = (half_tau * wave + jnp.where(same, -half_tau, half_tau)).astype(jnp.bfloat16)

    def img_grads(i0, n):
        img.store(lax.dot_general(coef[:, i0:i0 + n], q_rows[...], TN, preferred_element_type=jnp.float32), i0)

    def txt_grads(t0, n):
        txt.store(lax.dot_general(coef[t0:t0 + n, :], p_rows[...], NN, preferred_element_type=jnp.float32), t0)

    sides = {"i": img, "t": txt}
    for step in PLAN:
        if step[0] == "send" and (step[1] != "i" or step[2:] not in img.sent):
            sides[step[1]].send(step[2:])
        elif step[0] == "send":
            pass
        elif step[0] == "give":
            sides[step[1]].give(step[2:])
        elif step[0] == "coef":
            scores(*step[1:])
        elif step[0] == "own":
            assert ("coef", 0, 384, 0, 384) in PLAN[: PLAN.index(step)]
            own_scores()
        elif step[0] == "img":
            img_grads(*step[1:])
        else:
            txt_grads(*step[1:])

    for side in (img, txt):
        side.settle()
        side.take(last=False)
    for side, unit, inverse, out in ((img, img_unit, img_inv, img_out), (txt, txt_unit, txt_inv, txt_out)):
        side.take(last=True)
        out[...] = back_norm(unit[...], inverse[:, 0:1], side.part[0:ROWS, :])
    img.finish()
    txt.finish()


def store_kernel(img_ref, txt_ref, img_out, txt_out, sems):
    stores = [
        pltpu.make_async_copy(here, there, sems.at[i])
        for i, (here, there) in enumerate(((img_ref, img_out), (txt_ref, txt_out)))
    ]
    for store in stores:
        store.start()
    for store in stores:
        store.wait()


def on_device(image_emb, text_emb, log_temp, bias):
    rows, width = image_emb.shape
    group = 16 * rows
    n_img, n_txt = len(img_edges()), len(txt_edges())
    vmem = pl.BlockSpec(memory_space=pltpu.VMEM)
    hbm = pl.BlockSpec(memory_space=pltpu.HBM)
    grads = pl.pallas_call(
        kernel,
        out_shape=[pltpu.VMEM((rows, width), jnp.float32)] * 2,
        in_specs=[pl.BlockSpec(memory_space=pl.ANY)] * 4,
        out_specs=[vmem, vmem],
        scratch_shapes=(
            [pltpu.VMEM((rows, width), jnp.bfloat16)] * 2
            + [pltpu.VMEM((1,), jnp.float32)] * 2
            + [pltpu.SemaphoreType.DMA((4,))]
            + [pltpu.VMEM((rows, width), jnp.float32)] * 2
            + [pltpu.VMEM((rows, 128), jnp.float32)] * 2
            + [pltpu.VMEM((group, width), jnp.bfloat16)] * 2
            + [pltpu.VMEM((group, group), jnp.bfloat16)]
            + [pltpu.VMEM((group, width), jnp.float32)] * 2
            + [pltpu.VMEM((group, width), jnp.bfloat16)] * 4
            + [pltpu.SemaphoreType.DMA((n_img,))] * 4
            + [pltpu.SemaphoreType.DMA((n_txt,))] * 4
        ),
        compiler_params=pltpu.CompilerParams(
            collective_id=0, has_side_effects=True, vmem_limit_bytes=56 * 2**20
        ),
    )(image_emb, text_emb, log_temp, bias)
    anywhere = pl.BlockSpec(memory_space=pl.ANY)
    return pl.pallas_call(
        store_kernel,
        out_shape=[jax.ShapeDtypeStruct((rows, width), jnp.float32)] * 2,
        in_specs=[vmem] * 2,
        out_specs=[anywhere] * 2,
        scratch_shapes=[pltpu.SemaphoreType.DMA((2,))],
    )(*(pltpu.with_memory_space_constraint(grad, pltpu.VMEM) for grad in grads))


def solution(mesh):
    placed = (P(("dp", "mp"), None), P(("dp", "mp"), None), P(), P())
    return jax.shard_map(
        on_device,
        mesh=mesh,
        in_specs=placed,
        out_specs=(P(("dp", "mp"), None), P(("dp", "mp"), None)),
        check_vma=False,
    )
```

```python
import functools

import jax
import jax.numpy as jnp
from jax import lax
from jax.experimental import pallas as pl
from jax.experimental.pallas import tpu as pltpu
from jax.sharding import PartitionSpec as P

EPS = 1e-06
MESH = pl.DeviceIdType.MESH
NX, NY, NZ = 4, 4, 8
ROWS = 64
HALF = ROWS // 2
QUARTER = ROWS // 4
NT = (((1,), (1,)), ((), ()))
TN = (((0,), (0,)), ((), ()))
NN = (((1,), (0,)), ((), ()))
CHUNKS = {1: (0, 1, 2, 3), -1: (2, 3, 0, 1)}

IMG_UNITS = (
    [((0, 0), 0), ((0, 0), 1)]
    + [((d, 0), 0) for d in (1, 3)] + [((0, d), 1) for d in (1, 3)]
    + [((0, d), 0) for d in (1, 3)] + [((d, 0), 1) for d in (1, 3)]
    + [((2, 0), 0), ((0, 2), 1)]
    + [((3, d), 0) for d in (1, 3)] + [((d, 3), 1) for d in (1, 3)]
    + [((1, d), 0) for d in (1, 3)] + [((d, 1), 1) for d in (1, 3)]
    + [((2, d), 0) for d in (1, 3)] + [((d, 2), 1) for d in (1, 3)]
    + [((0, 2), 0), ((2, 0), 1)]
    + [((3, 2), 0), ((2, 3), 1), ((1, 2), 0), ((2, 1), 1), ((2, 2), 0), ((2, 2), 1)]
)
TXT_UNITS = [((dz, s), 0) for dz in (0, 1, 7, 2, 6, 3, 5, 4) for s in (0, 1)]


PLAN = (
    ("send", "t", "z", 0, -1, 2), ("send", "t", "z", 0, 1, 0), ("send", "t", "z", 0, -1, 3),
    ("send", "i", "f", "A", 0, 1, 0), ("send", "i", "f", "B", 0, -1, 0), ("send", "t", "z", 0, 1, 1),
    ("send", "i", "f", "B", 0, 1, 0), ("send", "i", "f", "A", 0, -1, 0), ("send", "t", "z", 0, -1, 0),
    ("send", "i", "f", "A", 0, 1, 1), ("send", "t", "z", 0, 1, 3), ("send", "i", "s", "A", 0, -1, 0),
    ("send", "i", "s", "B", 0, -1, 1), ("send", "t", "z", 0, 1, 2), ("send", "i", "f", "B", 0, -1, 1),
    ("send", "i", "s", "B", 0, 1, 0), ("send", "i", "s", "A", 0, 1, 1), ("send", "i", "f", "B", 0, 1, 1),
    ("send", "i", "s", "A", 0, 1, 0), ("send", "i", "s", "B", 0, 1, 1), ("send", "i", "f", "A", 0, -1, 1),
    ("send", "i", "s", "B", 0, -1, 0), ("send", "i", "s", "A", 0, -1, 1), ("send", "t", "z", 0, -1, 1),
    ("send", "t", "z", 1, -1, 2), ("send", "t", "z", 1, 1, 0), ("send", "i", "fq", "A", 0, 1, 0),
    ("send", "i", "fq", "B", 0, -1, 0), ("send", "i", "s", "A", 1, -1, 0), ("send", "i", "fq", "A", 0, -1, 0),
    ("send", "i", "fq", "B", 0, 1, 0), ("send", "i", "s", "B", 1, 1, 1), ("send", "i", "s", "B", 3, -1, 1),
    ("send", "t", "z", 1, -1, 3), ("send", "t", "z", 1, 1, 1), ("send", "i", "s", "B", 3, 1, 0),
    ("send", "i", "sq", "A", 0, -1, 0), ("send", "i", "s", "B", 1, -1, 0), ("send", "i", "s", "A", 3, 1, 0),
    ("send", "t", "z", 1, -1, 0), ("send", "i", "sq", "B", 0, 1, 0), ("send", "t", "c", 1, 1),
    ("send", "t", "z", 1, 1, 3), ("send", "t", "c", 7, 0), ("send", "i", "s", "B", 3, -1, 0),
    ("send", "i", "s", "B", 3, 1, 1), ("send", "i", "s", "A", 1, 1, 1), ("send", "i", "s", "A", 1, 1, 0),
    ("send", "i", "s", "A", 3, -1, 0), ("send", "i", "s", "B", 1, -1, 1), ("send", "t", "z", 1, -1, 1),
    ("send", "i", "s", "A", 1, -1, 1), ("send", "t", "z", 1, 1, 2), ("send", "i", "s", "A", 3, -1, 1),
    ("send", "t", "c", 7, 1), ("send", "t", "z", 2, -1, 2), ("send", "t", "z", 2, 1, 0),
    ("send", "i", "s", "A", 2, 1, 0), ("send", "i", "s", "B", 2, 1, 0), ("send", "t", "c", 0, 0),
    ("send", "i", "s", "A", 3, 1, 1), ("send", "t", "z", 2, -1, 3), ("send", "t", "z", 2, 1, 1),
    ("send", "t", "c", 0, 1), ("send", "t", "c", 2, 1), ("send", "i", "s", "B", 2, -1, 0),
    ("send", "i", "s", "A", 2, -1, 0), ("send", "t", "c", 6, 0), ("send", "i", "sq", "A", 3, 1, 0),
    ("send", "t", "c", 1, 0), ("send", "i", "s", "B", 1, 1, 0), ("send", "t", "z", 2, -1, 0),
    ("send", "i", "s", "B", 2, -1, 1), ("send", "i", "sq", "B", 3, 1, 0), ("send", "t", "z", 2, 1, 3),
    ("send", "i", "sq", "B", 0, -1, 0), ("send", "i", "s", "A", 2, -1, 1), ("send", "t", "z", 2, -1, 1),
    ("send", "i", "sq", "A", 3, -1, 0), ("send", "i", "s", "B", 2, 1, 1), ("send", "i", "sq", "A", 0, 1, 0),
    ("send", "t", "z", 2, 1, 2), ("coef", 0, 384, 0, 384), ("send", "i", "sq", "B", 3, -1, 0),
    ("send", "i", "sq", "A", 1, -1, 0), ("send", "i", "s", "A", 2, 1, 1), ("send", "i", "sq", "B", 1, -1, 0),
    ("send", "i", "sq", "A", 1, 1, 0), ("send", "t", "c", 2, 0), ("send", "t", "z", 3, -1, 2),
    ("send", "t", "z", 3, 1, 0), ("send", "i", "sq", "B", 2, 1, 0), ("send", "i", "sq", "A", 2, 1, 0),
    ("send", "t", "z", 3, -1, 3), ("send", "t", "z", 3, 1, 1), ("send", "t", "c", 5, 0), ("send", "t", "c", 6, 1),
    ("send", "t", "c", 3, 1), ("send", "i", "sq", "B", 1, 1, 0), ("send", "i", "sq", "B", 2, -1, 0),
    ("send", "i", "sq", "A", 2, -1, 0), ("coef", 0, 384, 384, 256), ("send", "t", "c", 3, 0),
    ("send", "t", "c", 5, 1), ("coef", 384, 256, 0, 640), ("own",), ("coef", 640, 256, 0, 896),
    ("send", "t", "c", 4, 1), ("send", "t", "c", 4, 0), ("coef", 0, 640, 640, 256), ("coef", 0, 896, 896, 128),
    ("coef", 896, 128, 0, 1024), ("txt", 896, 128), ("give", "t", "c", 4, 0), ("give", "t", "c", 4, 1),
    ("img", 896, 128), ("give", "i", "sq", "A", 2, -1, 0), ("give", "i", "sq", "B", 2, -1, 0),
    ("give", "i", "sq", "A", 2, 1, 0), ("give", "i", "sq", "B", 2, 1, 0), ("give", "i", "sq", "A", 1, 1, 0),
    ("img", 768, 128), ("give", "i", "sq", "B", 1, 1, 0), ("give", "i", "sq", "B", 1, -1, 0),
    ("give", "t", "z", 3, 1, 0), ("give", "i", "sq", "A", 1, -1, 0), ("give", "t", "z", 3, -1, 2), ("txt", 640, 256),
    ("give", "t", "c", 5, 1), ("give", "t", "z", 3, -1, 3), ("give", "t", "z", 3, 1, 1), ("give", "t", "c", 3, 0),
    ("give", "i", "sq", "B", 3, 1, 0), ("give", "i", "sq", "A", 3, 1, 0), ("give", "i", "sq", "A", 3, -1, 0),
    ("give", "i", "sq", "B", 3, -1, 0), ("img", 512, 256), ("give", "t", "z", 2, 1, 2), ("give", "t", "z", 2, -1, 0),
    ("give", "i", "s", "A", 2, 1, 1), ("give", "t", "z", 2, -1, 1), ("give", "t", "c", 3, 1),
    ("give", "i", "s", "B", 2, 1, 1), ("give", "t", "z", 2, 1, 3), ("give", "t", "c", 5, 0),
    ("give", "i", "s", "A", 2, -1, 1), ("give", "i", "s", "B", 2, -1, 1), ("txt", 384, 256),
    ("give", "i", "s", "A", 2, -1, 0), ("give", "i", "s", "A", 2, 1, 0), ("give", "i", "s", "B", 2, -1, 0),
    ("give", "i", "s", "B", 2, 1, 0), ("give", "i", "sq", "B", 0, 1, 0), ("give", "i", "sq", "A", 0, 1, 0),
    ("give", "t", "c", 2, 0), ("give", "i", "s", "A", 1, -1, 1), ("give", "i", "sq", "B", 0, -1, 0),
    ("give", "t", "z", 2, 1, 0), ("give", "i", "sq", "A", 0, -1, 0), ("give", "t", "z", 2, -1, 2), ("img", 256, 256),
    ("give", "t", "z", 2, -1, 3), ("give", "t", "z", 2, 1, 1), ("give", "i", "s", "A", 1, 1, 0),
    ("give", "i", "s", "B", 3, 1, 1), ("give", "i", "s", "B", 1, -1, 1), ("give", "t", "c", 6, 1),
    ("give", "i", "s", "B", 3, 1, 0), ("txt", 128, 256), ("give", "i", "s", "A", 3, -1, 1),
    ("give", "i", "s", "A", 1, 1, 1), ("give", "i", "s", "B", 3, -1, 1), ("give", "t", "c", 6, 0),
    ("give", "i", "s", "B", 1, 1, 0), ("give", "t", "z", 1, -1, 0), ("give", "t", "z", 1, 1, 2),
    ("give", "i", "s", "A", 1, -1, 0), ("give", "i", "s", "A", 3, 1, 0), ("give", "i", "s", "A", 3, 1, 1),
    ("give", "i", "s", "A", 3, -1, 0), ("give", "i", "s", "B", 3, -1, 0), ("give", "t", "c", 2, 1),
    ("give", "i", "s", "B", 1, 1, 1), ("give", "i", "s", "B", 1, -1, 0), ("give", "t", "z", 1, 1, 3),
    ("give", "t", "z", 1, -1, 1), ("img", 0, 256), ("give", "t", "z", 1, -1, 2), ("give", "t", "z", 1, 1, 0),
    ("give", "i", "fq", "B", 0, -1, 0), ("give", "t", "c", 1, 0), ("give", "i", "fq", "A", 0, -1, 0),
    ("give", "i", "fq", "A", 0, 1, 0), ("give", "i", "fq", "B", 0, 1, 0), ("give", "i", "s", "A", 0, 1, 1),
    ("give", "i", "s", "B", 0, 1, 1), ("give", "t", "c", 7, 0), ("give", "t", "c", 1, 1), ("give", "t", "c", 7, 1),
    ("give", "t", "z", 1, -1, 3), ("give", "t", "z", 1, 1, 1), ("give", "i", "s", "B", 0, 1, 0), ("txt", 0, 128),
    ("give", "i", "s", "A", 0, -1, 0), ("give", "i", "s", "A", 0, 1, 0), ("give", "i", "f", "A", 0, -1, 1),
    ("give", "i", "s", "B", 0, -1, 1), ("give", "t", "z", 0, -1, 0), ("give", "t", "z", 0, 1, 2),
    ("give", "t", "c", 0, 0), ("give", "i", "s", "A", 0, -1, 1), ("give", "t", "z", 0, -1, 1),
    ("give", "t", "z", 0, 1, 3), ("give", "t", "c", 0, 1), ("give", "i", "f", "B", 0, -1, 1),
    ("give", "i", "f", "A", 0, 1, 1), ("give", "i", "f", "B", 0, 1, 1), ("give", "i", "s", "B", 0, -1, 0),
    ("give", "t", "z", 0, -1, 2), ("give", "t", "z", 0, 1, 0), ("give", "i", "f", "B", 0, -1, 0),
    ("give", "i", "f", "B", 0, 1, 0), ("give", "i", "f", "A", 0, -1, 0), ("give", "i", "f", "A", 0, 1, 0),
    ("give", "t", "z", 0, -1, 3), ("give", "t", "z", 0, 1, 1),
)

class Edge:
    def __init__(self, src, dst, row, count, axis, sign):
        self.src, self.dst, self.row, self.count = src, dst, row, count
        self.axis, self.sign = axis, sign


def img_edges():
    edges = {}
    for half, first, second in (("A", "x", "y"), ("B", "y", "x")):
        base = 0 if half == "A" else HALF

        def at(df, ds, first=first):
            return (df % 4, ds % 4) if first == "x" else (ds % 4, df % 4)

        for sg in (1, -1):
            rows = (base, base + QUARTER) if sg == 1 else (base + QUARTER, base)
            for i in (0, 1):
                edges["f", half, 0, sg, i] = Edge(at(0, 0), at(-sg, 0), rows[i], QUARTER, first, sg)
            edges["fq", half, 0, sg, 0] = Edge(at(-sg, 0), at(2, 0), rows[0], QUARTER, first, sg)
            for df in range(4):
                for i in (0, 1):
                    edges["s", half, df, sg, i] = Edge(at(df, 0), at(df, -sg), rows[i], QUARTER, second, sg)
                edges["sq", half, df, sg, 0] = Edge(at(df, -sg), at(df, 2), rows[0], QUARTER, second, sg)
    return edges


def txt_edges():
    edges = {}
    for sg in (1, -1):
        for k in range(4):
            for c in CHUNKS[sg][: 4 if k < 3 else 2]:
                edges["z", k, sg, c] = Edge(
                    ((-sg * k) % NZ, 0), ((-sg * (k + 1)) % NZ, 0), c * QUARTER, QUARTER, "z", sg
                )
    for dz in range(NZ):
        for h in (0, 1):
            edges["c", dz, h] = Edge((dz, 0), (dz, 1), h * HALF, HALF, "c", 1)
    return edges


class Side:
    def __init__(self, units, edges, rows, part, out, back, sems, place):
        self.unit = 16 * ROWS // len(units)
        self.at = {unit: i * self.unit for i, unit in enumerate(units)}
        self.done = set()
        self.edges = edges
        self.number = {key: i for i, key in enumerate(edges)}
        self.rows, self.part, self.out, self.back = rows, part, out, back
        self.g_send, self.g_recv, self.r_send, self.r_recv = sems
        self.place = place
        self.sent, self.returned = set(), set()
        self.seen, self.taken = set(), set()

    def span(self, slot, row, count):
        return pl.ds(self.at[slot, row // self.unit] + row % self.unit, count)

    def gather_copy(self, key):
        e, i = self.edges[key], self.number[key]
        return pltpu.make_async_remote_copy(
            src_ref=self.rows.at[self.span(e.src, e.row, e.count)],
            dst_ref=self.rows.at[self.span(e.dst, e.row, e.count)],
            send_sem=self.g_send.at[i],
            recv_sem=self.g_recv.at[i],
            device_id=self.place(e.axis, e.sign),
            device_id_type=MESH,
        )

    def scatter_copy(self, key):
        e, i = self.edges[key], self.number[key]
        where = self.span(e.dst, e.row, e.count)
        return pltpu.make_async_remote_copy(
            src_ref=self.out.at[where],
            dst_ref=self.back.at[where],
            send_sem=self.r_send.at[i],
            recv_sem=self.r_recv.at[i],
            device_id=self.place(e.axis, -e.sign),
            device_id_type=MESH,
        )

    def send(self, *keys):
        for key in keys:
            e = self.edges[key]
            self.arrive(e.src, e.row, e.count)
            self.gather_copy(key).start()
            self.sent.add(key)

    def arrive_until(self, end):
        for (slot, which), start in self.at.items():
            if start < end:
                self.arrive(slot, which * self.unit, self.unit)

    def arrive(self, slot, row=0, count=ROWS):
        for key, e in self.edges.items():
            if e.dst == slot and e.row < row + count and row < e.row + e.count and key not in self.seen:
                assert key in self.sent, key
                self.gather_copy(key).wait_recv()
                self.seen.add(key)

    def total(self, slot, row, count):
        assert self.span(slot, row, count).start in self.done
        value = self.part[self.span(slot, row, count), :]
        for key, e in self.edges.items():
            if e.src == slot and e.row <= row and row + count <= e.row + e.count:
                if key not in self.taken:
                    assert key in self.returned, key
                    self.scatter_copy(key).wait_recv()
                    self.taken.add(key)
                value = value + self.back[self.span(e.dst, row, count), :].astype(jnp.float32)
        return value

    def passed(self, slot, row):
        return any(e.src == slot and e.row <= row < e.row + e.count for e in self.edges.values())

    def store(self, value, start):
        for (slot, which), first in self.at.items():
            if not start <= first < start + value.shape[0]:
                continue
            for row in range(0, self.unit, QUARTER):
                at = first + row
                rows = value[at - start:at - start + QUARTER, :]
                if self.passed(slot, which * self.unit + row):
                    self.part[at:at + QUARTER, :] = rows
                else:
                    self.out[at:at + QUARTER, :] = rows.astype(jnp.bfloat16)
                self.done.add(at)

    def give(self, *keys):
        for key in keys:
            e = self.edges[key]
            for row in range(e.row, e.row + e.count, QUARTER):
                where = self.span(e.dst, row, QUARTER)
                assert where.start in self.done
                if self.passed(e.dst, row):
                    self.out[where, :] = self.total(e.dst, row, QUARTER).astype(jnp.bfloat16)
            self.scatter_copy(key).start()
            self.returned.add(key)

    def take(self, last):
        own = {
            key: e for key, e in self.edges.items() if e.src == (0, 0) and (key[0] in ("f", "z")) == last
        }
        for key in own:
            assert key in self.returned
            self.scatter_copy(key).wait_recv()
            self.taken.add(key)
        for row in range(0, ROWS, QUARTER):
            value = self.part[self.span((0, 0), row, QUARTER), :]
            for e in own.values():
                if e.row <= row and row + QUARTER <= e.row + e.count:
                    value = value + self.back[self.span(e.dst, row, QUARTER), :].astype(jnp.float32)
            self.part[self.span((0, 0), row, QUARTER), :] = value

    def settle(self):
        for key in self.edges:
            self.gather_copy(key).wait_send()
            if self.edges[key].src != (0, 0):
                self.scatter_copy(key).wait_send()

    def finish(self):
        assert len(self.sent) == len(self.returned) == len(self.seen) == len(self.taken) == len(self.edges)
        for key in self.edges:
            if self.edges[key].src == (0, 0):
                self.scatter_copy(key).wait_send()


def unit_of(emb):
    wide = emb.astype(jnp.float32)
    inverse = lax.rsqrt(jnp.sum(wide * wide, axis=1, keepdims=True) + EPS)
    return wide * inverse, inverse


def back_norm(unit, inverse, grad):
    return inverse * (grad - unit * jnp.sum(unit * grad, axis=1, keepdims=True))


def kernel(
    img_hbm, txt_hbm, temp_hbm, bias_hbm, img_out, txt_out,
    img_ref, txt_ref, temp_ref, bias_ref, in_sems, img_unit, txt_unit, img_inv, txt_inv,
    p_rows, q_rows, coef, p_part, q_part, p_send, q_send, p_back, q_back,
    pg_send, pg_recv, pr_send, pr_recv, qg_send, qg_recv, qr_send, qr_recv,
):
    dp, mp = lax.axis_index("dp"), lax.axis_index("mp")
    core, z, x = dp % 2, (dp // 2) % NZ, (dp // (2 * NZ)) * 2 + mp // NY
    y = mp % NY

    @functools.cache
    def place(axis, sign):
        nx, ny, nz, nc = x, y, z, core
        if axis == "x":
            nx = (x + sign + NX) % NX
        elif axis == "y":
            ny = (y + sign + NY) % NY
        elif axis == "z":
            nz = (z + sign + NZ) % NZ
        else:
            nc = 1 - core
        return ((nx // 2) * (2 * NZ) + nz * 2 + nc, (nx % 2) * NY + ny)

    barrier = pltpu.get_barrier_semaphore()
    neighbours = [place(a, s) for a in "xyz" for s in (1, -1)] + [place("c", 1)]
    for device in neighbours:
        pl.semaphore_signal(barrier, inc=1, device_id=device, device_id_type=MESH)

    loads = [
        pltpu.make_async_copy(here, there, in_sems.at[i])
        for i, (here, there) in enumerate(
            ((img_hbm, img_ref), (txt_hbm, txt_ref), (temp_hbm, temp_ref), (bias_hbm, bias_ref))
        )
    ]
    for load in loads:
        load.start()
    img = Side(IMG_UNITS, img_edges(), p_rows, p_part, p_send, p_back,
               (pg_send, pg_recv, pr_send, pr_recv), place)
    txt = Side(TXT_UNITS, txt_edges(), q_rows, q_part, q_send, q_back,
               (qg_send, qg_recv, qr_send, qr_recv), place)

    loads[0].wait()
    unit, inverse = unit_of(img_ref[...])
    p_rows[0:ROWS, :] = unit.astype(jnp.bfloat16)
    img_unit[...] = unit
    img_inv[...] = jnp.broadcast_to(inverse, img_inv.shape)
    pl.semaphore_wait(barrier, len(neighbours))
    for sg in (1, -1):
        for half in "AB":
            img.send(("f", half, 0, sg, 0))
    for load in loads[1:]:
        load.wait()
    half_tau = 0.5 * jnp.exp(temp_ref[...].reshape(1, 1))
    half_bias = 0.5 * bias_ref[...].reshape(1, 1)

    unit, inverse = unit_of(txt_ref[...])
    q_rows[0:ROWS, :] = unit.astype(jnp.bfloat16)
    txt_unit[...] = unit
    txt_inv[...] = jnp.broadcast_to(inverse, txt_inv.shape)

    def scores(t0, tn, i0, n):
        txt.arrive_until(t0 + tn)
        img.arrive_until(i0 + n)
        dots = lax.dot_general(q_rows[t0:t0 + tn, :], p_rows[i0:i0 + n, :], NT,
                               preferred_element_type=jnp.float32)
        wave = jnp.tanh(half_tau * dots + half_bias)
        coef[t0:t0 + tn, i0:i0 + n] = (half_tau * wave + half_tau).astype(jnp.bfloat16)

    def own_scores():
        dots = lax.dot_general(q_rows[0:ROWS, :], p_rows[0:128, :], NT,
                               preferred_element_type=jnp.float32)
        wave = jnp.tanh(half_tau * dots + half_bias)
        same = lax.broadcasted_iota(jnp.int32, dots.shape, 0) == lax.broadcasted_iota(jnp.int32, dots.shape, 1)
        coef[0:ROWS, 0:128] = (half_tau * wave + jnp.where(same, -half_tau, half_tau)).astype(jnp.bfloat16)

    def img_grads(i0, n):
        img.store(lax.dot_general(coef[:, i0:i0 + n], q_rows[...], TN, preferred_element_type=jnp.float32), i0)

    def txt_grads(t0, n):
        txt.store(lax.dot_general(coef[t0:t0 + n, :], p_rows[...], NN, preferred_element_type=jnp.float32), t0)

    sides = {"i": img, "t": txt}
    for step in PLAN:
        if step[0] == "send" and (step[1] != "i" or step[2:] not in img.sent):
            sides[step[1]].send(step[2:])
        elif step[0] == "send":
            pass
        elif step[0] == "give":
            sides[step[1]].give(step[2:])
        elif step[0] == "coef":
            scores(*step[1:])
        elif step[0] == "own":
            assert ("coef", 0, 384, 0, 384) in PLAN[: PLAN.index(step)]
            own_scores()
        elif step[0] == "img":
            img_grads(*step[1:])
        else:
            txt_grads(*step[1:])

    for side in (img, txt):
        side.settle()
        side.take(last=False)
    for side, unit, inverse, out in ((img, img_unit, img_inv, img_out), (txt, txt_unit, txt_inv, txt_out)):
        side.take(last=True)
        out[...] = back_norm(unit[...], inverse[:, 0:1], side.part[0:ROWS, :])
    img.finish()
    txt.finish()


def store_kernel(img_ref, txt_ref, img_out, txt_out, sems):
    stores = [
        pltpu.make_async_copy(here.at[pl.ds(row, QUARTER)], there.at[pl.ds(row, QUARTER)], sems.at[i, row // QUARTER])
        for i, (here, there) in enumerate(((img_ref, img_out), (txt_ref, txt_out)))
        for row in range(0, ROWS, QUARTER)
    ]
    for store in stores:
        store.start()
    for store in stores:
        store.wait()


def on_device(image_emb, text_emb, log_temp, bias):
    rows, width = image_emb.shape
    group = 16 * rows
    n_img, n_txt = len(img_edges()), len(txt_edges())
    vmem = pl.BlockSpec(memory_space=pltpu.VMEM)
    hbm = pl.BlockSpec(memory_space=pltpu.HBM)
    grads = pl.pallas_call(
        kernel,
        out_shape=[pltpu.VMEM((rows, width), jnp.float32)] * 2,
        in_specs=[pl.BlockSpec(memory_space=pl.ANY)] * 4,
        out_specs=[vmem, vmem],
        scratch_shapes=(
            [pltpu.VMEM((rows, width), jnp.bfloat16)] * 2
            + [pltpu.VMEM((1,), jnp.float32)] * 2
            + [pltpu.SemaphoreType.DMA((4,))]
            + [pltpu.VMEM((rows, width), jnp.float32)] * 2
            + [pltpu.VMEM((rows, 128), jnp.float32)] * 2
            + [pltpu.VMEM((group, width), jnp.bfloat16)] * 2
            + [pltpu.VMEM((group, group), jnp.bfloat16)]
            + [pltpu.VMEM((group, width), jnp.float32)] * 2
            + [pltpu.VMEM((group, width), jnp.bfloat16)] * 4
            + [pltpu.SemaphoreType.DMA((n_img,))] * 4
            + [pltpu.SemaphoreType.DMA((n_txt,))] * 4
        ),
        compiler_params=pltpu.CompilerParams(
            collective_id=0, has_side_effects=True, vmem_limit_bytes=56 * 2**20
        ),
    )(image_emb, text_emb, log_temp, bias)
    anywhere = pl.BlockSpec(memory_space=pl.ANY)
    return pl.pallas_call(
        store_kernel,
        out_shape=[jax.ShapeDtypeStruct((rows, width), jnp.float32)] * 2,
        in_specs=[vmem] * 2,
        out_specs=[anywhere] * 2,
        scratch_shapes=[pltpu.SemaphoreType.DMA((2, ROWS // QUARTER))],
    )(*(pltpu.with_memory_space_constraint(grad, pltpu.VMEM) for grad in grads))


def solution(mesh):
    placed = (P(("dp", "mp"), None), P(("dp", "mp"), None), P(), P())
    return jax.shard_map(
        on_device,
        mesh=mesh,
        in_specs=placed,
        out_specs=(P(("dp", "mp"), None), P(("dp", "mp"), None)),
        check_vma=False,
    )
```
